256 devices in a mesh: ctx: 32 (over z, x), ch: 8 (over y, core).
Axes of the slice: x: 4, y: 4, z: 8, core: 2. Of those that a mesh axis runs over, the one named last changes fastest.
Arguments:
- gate_signal: bfloat16 [8192, 4096], P('ctx', 'ch'), may hold values from -6 to 6
- key_signal: bfloat16 [8192, 4096], P('ctx', 'ch'), may hold values from -6 to 6
- value_signal: bfloat16 [8192, 4096], P('ctx', 'ch'), may hold values from -6 to 6
- pole_decay: float32 [16, 4096], P(None, 'ch'), may hold values from 0 to 1, as said below
- pole_angle: float32 [16, 4096], P(None, 'ch'), may hold values from -3.140625 to 3.140625
- residue_real: float32 [16, 4096], P(None, 'ch'), may hold values from -1 to 1
- residue_imag: float32 [16, 4096], P(None, 'ch'), may hold values from -1 to 1
- skip_gain: float32 [4096], P('ch'), may hold values from -4 to 4
- out_weight: bfloat16 [4096, 4096], P(None, 'ch'), may hold values from -0.09375 to 0.09375
Outputs:
- mixer_out: bfloat16 [8192, 4096], P('ctx', 'ch')
The draws below stay inside these ranges and needn't reach their ends.
Inputs may be any that keep to these rules, and one draw needn't show every extreme that they name: `pole_decay`: every entry is positive.
All inputs are finite; a program needn't handle non-finite values.
Results may differ from the reference program's by a relative error of at most 0.019.
Values may be sent and summed in bfloat16 or wider, within the bound.
A program may use at most 128 MiB of HBM per device.

```python
import jax
import jax.numpy as jnp
from jax import lax

D = 4096
MODES = 16
BLOCK = 64
TOKENS = 8192


def shared_decay(key, fast_share):
    mask_key, slow_key, quick_key = jax.random.split(key, 3)
    quick_mask = jax.random.uniform(mask_key, (1, D)) < fast_share
    slow_rate = jnp.exp(jax.random.uniform(slow_key, (MODES, D), minval=jnp.log(0.3 / TOKENS), maxval=jnp.log(2.0 / TOKENS)))
    quick_rate = jnp.exp(jax.random.uniform(quick_key, (MODES, D), minval=jnp.log(1.0 / 50.0), maxval=jnp.log(1.0 / 30.0)))
    return jnp.where(quick_mask, quick_rate, slow_rate)


def scaled_residue(key, decays):
    if_normal = jnp.clip(jax.random.normal(key, (MODES, D)), -4.0, 4.0)
    base_value = if_normal
    return base_value * jnp.sqrt((1.0 - jnp.exp(-2.0 * decays)) / MODES)


def draw_pole_decay(key, part):
    fast_share = 0.5
    return shared_decay(key, fast_share)


def draw_residue_real(key, part):
    fast_share = 0.5
    decays = shared_decay(key, fast_share)
    key = jax.random.fold_in(key, 3)
    return scaled_residue(key, decays)


def draw_residue_imag(key, part):
    fast_share = 0.5
    decays = shared_decay(key, fast_share)
    key = jax.random.fold_in(key, 5)
    return scaled_residue(key, decays)


def levels(stream_key, extent, cuts, low, top_value):
    loudness, own = 1.0, jax.random.fold_in(stream_key, 6)
    for position, blocks in cuts:
        heights = jnp.exp(jax.random.uniform(jax.random.fold_in(own, position), (blocks,), jnp.float32, low / len(cuts), top_value / len(cuts)))
        loudness = loudness * jnp.repeat(heights, extent[position] // blocks).reshape([-1 if axis == position else 1 for axis in range(len(extent))])
    return loudness


def gaussian(own_key, shape, spread, limit, cuts=(), held_as=jnp.bfloat16):
    level = levels(own_key, shape, cuts, -0.22, 0.18) if cuts else 1.0
    values = jax.random.normal(own_key, shape, jnp.float32) * spread * level
    return jnp.minimum(jnp.maximum(values, -limit), limit).astype(held_as)


def setup_inputs(seed: int = 0) -> dict:
    splits = jax.random.split(jax.random.key(seed), 10)
    return {
        "gate_signal": gaussian(splits[0], (TOKENS, D), 1.0, 6.0, ((0, 32), (1, 8))),
        "key_signal": gaussian(splits[1], (TOKENS, D), 1.0, 6.0, ((0, 32), (1, 8))),
        "value_signal": gaussian(splits[2], (TOKENS, D), 1.0, 6.0, ((0, 32), (1, 8))),
        "pole_decay": draw_pole_decay(jax.random.fold_in(splits[9], 71), 0),
        "pole_angle": jnp.clip(jax.random.uniform(splits[4], (MODES, D), jnp.float32, -3.140625, 3.140625), -3.140625, 3.140625),
        "residue_real": draw_residue_real(jax.random.fold_in(splits[9], 71), 0),
        "residue_imag": draw_residue_imag(jax.random.fold_in(splits[9], 71), 0),
        "skip_gain": gaussian(splits[7], (D,), 1.0, 4.0, ((0, 8),), jnp.float32),
        "out_weight": gaussian(splits[8], (D, D), D ** -0.5, 0.09375, ((1, 8),)),
    }


PRECISE = lax.Precision.HIGHEST


def powers(decays, angles, exponent):
    magnitude = jnp.exp(-exponent * decays)
    return jnp.stack([magnitude * jnp.cos(exponent * angles), magnitude * jnp.sin(exponent * angles)])


def complex_mul(former, latter):
    return jnp.stack([former[0] * latter[0] - former[1] * latter[1], former[0] * latter[1] + former[1] * latter[0]])


def reference(gate_signal, key_signal, value_signal, pole_decay, pole_angle, residue_real, residue_imag, skip_gain, out_weight):
    driving = key_signal.astype(jnp.float32) * value_signal.astype(jnp.float32)
    count_blocks = TOKENS // BLOCK
    blocked = driving.reshape(count_blocks, BLOCK, D)
    offsets = jnp.arange(BLOCK).astype(jnp.float32)[:, None, None]
    powers_table = powers(pole_decay, pole_angle, offsets)
    response = jnp.sum(residue_real * powers_table[0] - residue_imag * powers_table[1], axis=1)
    lag_index = jnp.arange(BLOCK)[:, None] - jnp.arange(BLOCK)[None, :]
    toeplitz = jnp.where((lag_index >= 0)[:, :, None], response[jnp.clip(lag_index, 0, BLOCK - 1)], 0.0)
    inner_part = jnp.einsum("tsc,bsc->btc", toeplitz, blocked, precision=PRECISE)
    block_sums = jnp.einsum("kjmc,bjc->kbmc", powers_table[:, ::-1], blocked, precision=PRECISE)
    ahead_pow = powers(pole_decay, pole_angle, offsets + 1.0)
    kernel = jnp.stack([residue_real * ahead_pow[0] - residue_imag * ahead_pow[1],
                        -(residue_real * ahead_pow[1] + residue_imag * ahead_pow[0])])
    block_step = powers(pole_decay, pole_angle, float(BLOCK))

    def advance(current, addend):
        return complex_mul(block_step, current) + addend, current

    _, block_starts = lax.scan(advance, jnp.zeros((2, MODES, D), jnp.float32), jnp.moveaxis(block_sums, 1, 0))
    block_starts = jnp.moveaxis(block_starts, 0, 1)
    state_part = jnp.einsum("kjmc,kbmc->bjc", kernel, block_starts, precision=PRECISE)
    long_out = inner_part + state_part + skip_gain * blocked
    gated_out = (gate_signal.astype(jnp.float32) * long_out.reshape(TOKENS, D)).astype(jnp.bfloat16)
    return jnp.dot(gated_out, out_weight.T, preferred_element_type=jnp.float32).astype(jnp.bfloat16)
```

```python
import functools

import jax
import jax.numpy as jnp
from jax import lax
from jax.experimental import pallas as pl
from jax.experimental.pallas import tpu as pltpu
from jax.sharding import PartitionSpec as P

MESH = pl.DeviceIdType.MESH
MODES = 16
STATE = 2 * MODES
LANES = 128
BLOCKS = 8
NX = 4
NY = 4
GROUPS = 2


def cmul(ar, ai, br, bi):
    return ar * br - ai * bi, ar * bi + ai * br


def advanced(step, state):
    real, imag = cmul(step[:MODES], step[MODES:], state[:MODES], state[MODES:])
    return jnp.concatenate([real, imag], axis=0)


def kernel(
    nz,
    gate,
    key,
    value,
    decay,
    angle,
    res_real,
    res_imag,
    skip,
    weight,
    out,
    gate_v,
    key_v,
    value_v,
    decay_v,
    angle_v,
    real_v,
    imag_v,
    skip_v,
    w_own,
    w_sib,
    u,
    g_perm,
    power,
    ker,
    taps,
    lam_block,
    lam_span,
    lam_row,
    sums,
    tot,
    tot_in,
    row_tot,
    row_in,
    before,
    start_out,
    start_in,
    states,
    local,
    g_own,
    g_sib,
    far_out,
    far_in,
    up_out,
    up_in,
    down_out,
    down_in,
    up_part,
    down_part,
    own_part,
    final,
    load_sem,
    wsib_sem,
    tot_send,
    tot_recv,
    row_send,
    row_recv,
    start_send,
    start_recv,
    gsib_send,
    gsib_recv,
    far_send,
    far_recv,
    up_send,
    up_recv,
    down_send,
    down_recv,
):
    rows, width = key_v.shape
    step = rows // BLOCKS
    quarters = width // LANES
    group_rows = rows // GROUPS
    half = group_rows // 2
    ctx, ch = lax.axis_index("ctx"), lax.axis_index("ch")
    z, x = ctx // NX, lax.rem(ctx, NX)
    y, core = ch // 2, lax.rem(ch, 2)
    sibling = {"ctx": ctx, "ch": y * 2 + (1 - core)}
    y_up, y_down, y_far = (lax.rem(y + d, NY) for d in (1, NY - 1, 2))
    up_dev = {"ctx": ctx, "ch": y_up * 2 + core}
    down_dev = {"ctx": ctx, "ch": y_down * 2 + core}

    def remote(src, dst, send, recv, device):
        return pltpu.make_async_remote_copy(
            src_ref=src, dst_ref=dst, send_sem=send, recv_sem=recv, device_id=device, device_id_type=MESH
        )

    pairs = (
        (decay, decay_v),
        (angle, angle_v),
        (key, key_v),
        (value, value_v),
        (res_real, real_v),
        (res_imag, imag_v),
        (skip, skip_v),
        (gate, gate_v),
        (weight.at[:, core], w_own),
    )
    loads = [pltpu.make_async_copy(src, dst, load_sem.at[i]) for i, (src, dst) in enumerate(pairs)]
    for load in loads:
        load.start()

    barrier = pltpu.get_barrier_semaphore()
    peers = [sibling, up_dev, down_dev]
    peers += [{"ctx": z * NX + lax.rem(x + d, NX), "ch": ch} for d in range(1, NX)]
    peers += [{"ctx": lax.rem(z + d, nz) * NX + x, "ch": ch} for d in range(1, nz)]
    for peer in peers:
        pl.semaphore_signal(barrier, inc=1, device_id=peer, device_id_type=MESH)

    loads[0].wait()
    loads[1].wait()
    magnitude = jnp.exp(-decay_v[...])
    lam_r = magnitude * jnp.cos(angle_v[...])
    lam_i = magnitude * jnp.sin(angle_v[...])

    def lanes(q):
        return slice(q * LANES, (q + 1) * LANES)

    def store_power(j, carry):
        pr, pi = carry
        for q in range(quarters):
            power[q, j, :MODES, :] = pr[:, lanes(q)]
            power[q, j, MODES:, :] = pi[:, lanes(q)]
        return cmul(pr, pi, lam_r, lam_i)

    pr, pi = lax.fori_loop(0, step, store_power, (jnp.ones_like(lam_r), jnp.zeros_like(lam_r)))
    for q in range(quarters):
        power[q, step, :MODES, :] = pr[:, lanes(q)]
        power[q, step, MODES:, :] = pi[:, lanes(q)]
        lam_block[q, :MODES, :] = pr[:, lanes(q)]
        lam_block[q, MODES:, :] = pi[:, lanes(q)]
    for _ in range(3):
        pr, pi = cmul(pr, pi, pr, pi)
    for q in range(quarters):
        lam_span[q, :MODES, :] = pr[:, lanes(q)]
        lam_span[q, MODES:, :] = pi[:, lanes(q)]
    for _ in range(2):
        pr, pi = cmul(pr, pi, pr, pi)
    for q in range(quarters):
        lam_row[q, :MODES, :] = pr[:, lanes(q)]
        lam_row[q, MODES:, :] = pi[:, lanes(q)]

    loads[2].wait()
    loads[3].wait()
    for q in range(quarters):
        u[q, : 8 * BLOCKS, :] = jnp.zeros((8 * BLOCKS, LANES), jnp.float32)
        for b in range(BLOCKS):
            part = slice(b * step, (b + 1) * step)
            drive = key_v[part, lanes(q)].astype(jnp.float32) * value_v[part, lanes(q)].astype(jnp.float32)
            u[q, pl.ds(8 * BLOCKS + b, step, stride=BLOCKS), :] = drive

    pl.semaphore_wait(barrier, len(peers))
    w_copy = remote(weight.at[:, 1 - core], w_sib, wsib_sem.at[0], wsib_sem.at[1], sibling)
    w_copy.start()

    def total_of(i, _):
        q = lax.rem(x + 1 + i, NX)

        def add_token(j, acc):
            row = u[q, pl.ds(pl.multiple_of(8 * BLOCKS + j * BLOCKS, BLOCKS), BLOCKS), :]
            return tuple(acc[k] + power[q, step - 1 - j, pl.ds(k, 1), :] * row for k in range(STATE))

        acc = lax.fori_loop(
            0, step, add_token, tuple(jnp.zeros((BLOCKS, LANES), jnp.float32) for _ in range(STATE)), unroll=2
        )
        for k in range(STATE):
            sums[q, pl.ds(k, BLOCKS, stride=STATE), :] = acc[k]
        lam = lam_block[q]
        state = sums[q, :STATE, :]
        for b in range(1, BLOCKS):
            state = advanced(lam, state) + sums[q, b * STATE : (b + 1) * STATE, :]
        tot[q] = state

        @pl.when(i < NX - 1)
        def _():
            remote(
                tot.at[q], tot_in.at[x], tot_send.at[q], tot_recv.at[x], {"ctx": z * NX + q, "ch": ch}
            ).start()

        @pl.when(i == NX - 1)
        def _():
            tot_in[x] = state

        return 0

    lax.fori_loop(0, quarters, total_of, 0)

    for i in (4, 5, 6):
        loads[i].wait()
    for q in range(quarters):
        rr, ri = real_v[:, lanes(q)], imag_v[:, lanes(q)]
        taps[q, 0:1, :] = jnp.sum(rr, axis=0, keepdims=True) + skip_v[:, lanes(q)]

        def store_ker(j, _, q=q, rr=rr, ri=ri):
            p = power[q, j + 1]
            kr, ki = cmul(rr, ri, p[:MODES], p[MODES:])
            ker[q, j, :MODES, :] = kr
            ker[q, j, MODES:, :] = -ki
            taps[q, pl.ds(j + 1, 1), :] = jnp.sum(kr, axis=0, keepdims=True)
            return 0

        lax.fori_loop(0, step, store_ker, 0, unroll=4)

    for d in range(1, NX):
        src = lax.rem(x + d, NX)
        remote(tot.at[src], tot_in.at[src], tot_send.at[src], tot_recv.at[src], sibling).wait_recv()
    lam = lam_span[x]
    state = tot_in[0]
    for i in range(1, NX):
        state = advanced(lam, state) + tot_in[i]
    row_tot[...] = state

    def row_copy(d):
        return remote(
            row_tot, row_in.at[z], row_send.at[d], row_recv.at[z], {"ctx": lax.rem(z + d, nz) * NX + x, "ch": ch}
        )

    for d in range(1, nz):

        @pl.when(z + d < nz)
        def _():
            row_copy(d).start()

    loads[7].wait()
    chunk = 8 * BLOCKS

    def fir(q, _):
        for c in range(step // 8):
            acc = None
            for lag in range(8 * c + 8):
                begin = chunk + c * chunk - lag * BLOCKS
                term = taps[q, pl.ds(lag, 1), :] * u[q, begin : begin + chunk, :]
                acc = term if acc is None else acc + term
            local[q, c * chunk : (c + 1) * chunk, :] = acc
        return 0

    lax.fori_loop(0, quarters, fir, 0)
    for q in range(quarters):
        for b in range(BLOCKS):
            part = slice(b * step, (b + 1) * step)
            g_perm[q, pl.ds(b, step, stride=BLOCKS), :] = gate_v[part, lanes(q)].astype(jnp.float32)

    lam = lam_row[x]
    before[...] = jnp.zeros_like(before)
    for s in range(nz - 1):

        @pl.when(s < z)
        def _():
            remote(row_tot, row_in.at[s], row_send.at[0], row_recv.at[s], sibling).wait_recv()
            before[...] = advanced(lam, before[...]) + row_in[s]

    lam = lam_span[x]
    state = before[...]
    for i in range(NX):
        start_out[i] = state
        if i < NX - 1:
            state = advanced(lam, state) + tot_in[i]
    for d in range(1, NX):
        to = lax.rem(x + d, NX)
        remote(
            start_out.at[to], start_in.at[x], start_send.at[d], start_recv.at[x], {"ctx": z * NX + to, "ch": ch}
        ).start()
    start_in[x] = start_out[x]
    for d in range(1, NX):
        src = lax.rem(x + d, NX)
        remote(start_out.at[src], start_in.at[src], start_send.at[0], start_recv.at[src], sibling).wait_recv()

    for q in range(quarters):
        lam = lam_block[q]
        state = start_in[q]
        for b in range(BLOCKS):
            states[q, pl.ds(b, STATE, stride=BLOCKS), :] = state
            if b < BLOCKS - 1:
                state = advanced(lam, state) + sums[q, b * STATE : (b + 1) * STATE, :]

    def rows_of(g):
        return slice(g * group_rows, (g + 1) * group_rows)

    def gated(g):
        pairs_in_group = group_rows // (2 * BLOCKS)

        for q in range(quarters):
            held = [states[q, k * BLOCKS : (k + 1) * BLOCKS, :] for k in range(STATE)]

            def two_tokens(i, _, q=q, held=held):
                done = []
                for t in range(2):
                    j = 2 * i + t
                    at = pl.ds(pl.multiple_of(j * BLOCKS, BLOCKS), BLOCKS)
                    partial = [local[q, at, :], None, None, None]
                    for k in range(STATE):
                        term = ker[q, j, pl.ds(k, 1), :] * held[k]
                        partial[k % 4] = term if partial[k % 4] is None else partial[k % 4] + term
                    total = (partial[0] + partial[1]) + (partial[2] + partial[3])
                    done.append(total * g_perm[q, at, :])
                to = pl.ds(pl.multiple_of(i * 2 * BLOCKS, 2 * BLOCKS), 2 * BLOCKS)
                g_own[to, lanes(q)] = jnp.concatenate(done, axis=0).astype(jnp.bfloat16)
                return 0

            lax.fori_loop(g * pairs_in_group, (g + 1) * pairs_in_group, two_tokens, 0)

    def sib_copy(g):
        at = rows_of(g)
        return remote(g_own.at[at], g_sib.at[at], gsib_send.at[g], gsib_recv.at[g], sibling)

    def product(g, to):
        dims = (((1,), (1,)), ((), ()))
        mine = lax.dot_general(g_own[rows_of(g), :], w_own[to], dims, preferred_element_type=jnp.float32)
        theirs = lax.dot_general(g_sib[rows_of(g), :], w_sib[to], dims, preferred_element_type=jnp.float32)
        return mine + theirs

    low, high = slice(0, half), slice(half, group_rows)

    def far_copies(g):
        return (
            remote(far_out.at[g, low], far_in.at[g, low], far_send.at[g, 0], far_recv.at[g, 0], up_dev),
            remote(far_out.at[g, high], far_in.at[g, high], far_send.at[g, 1], far_recv.at[g, 1], down_dev),
        )

    def up_copy(g, i):
        at = (low, high)[i]
        return remote(up_out.at[g, at], up_in.at[g, at], up_send.at[g, i], up_recv.at[g, i], up_dev)

    def down_copy(g, i):
        at = (low, high)[i]
        return remote(down_out.at[g, at], down_in.at[g, at], down_send.at[g, i], down_recv.at[g, i], down_dev)

    def send_off(g):
        far_out[g] = product(g, y_far).astype(jnp.bfloat16)
        for copy in far_copies(g):
            copy.start()
        part = product(g, y_up)
        up_out[g, high] = part[half:].astype(jnp.bfloat16)
        up_copy(g, 1).start()
        up_part[...] = part[:half]
        part = product(g, y_down)
        down_out[g, low] = part[:half].astype(jnp.bfloat16)
        down_copy(g, 0).start()
        down_part[...] = part[half:]

    def send_rest(g):
        arrived = far_copies(g)
        arrived[0].wait_recv()
        up_out[g, low] = (up_part[...] + far_in[g, low].astype(jnp.float32)).astype(jnp.bfloat16)
        up_copy(g, 0).start()
        arrived[1].wait_recv()
        down_out[g, high] = (down_part[...] + far_in[g, high].astype(jnp.float32)).astype(jnp.bfloat16)
        down_copy(g, 1).start()
        own_part[rows_of(g), :] = product(g, y)

    for g in range(GROUPS):
        gated(g)
        sib_copy(g).start()
        if g == 0:
            loads[8].wait()
            w_copy.wait_recv()
        else:
            send_rest(g - 1)
        sib_copy(g).wait_recv()
        send_off(g)
    send_rest(GROUPS - 1)

    for g in range(GROUPS):
        for i in (1, 0):
            at = (low, high)[i]
            down_copy(g, 1 - i).wait_recv()
            up_copy(g, i).wait_recv()
        whole = own_part[rows_of(g), :] + up_in[g].astype(jnp.float32) + down_in[g].astype(jnp.float32)
        for q in range(quarters):
            final[q, rows_of(g), :] = whole[:, lanes(q)]
    for q in range(quarters):
        for b in range(BLOCKS):
            out[b * step : (b + 1) * step, lanes(q)] = final[q, pl.ds(b, step, stride=BLOCKS), :].astype(jnp.bfloat16)

    w_copy.wait_send()
    for d in range(1, NX):
        q = lax.rem(x + d, NX)
        remote(tot.at[q], tot_in.at[x], tot_send.at[q], tot_recv.at[x], sibling).wait_send()
        remote(start_out.at[q], start_in.at[x], start_send.at[d], start_recv.at[x], sibling).wait_send()
    for d in range(1, nz):

        @pl.when(z + d < nz)
        def _():
            row_copy(d).wait_send()

    for g in range(GROUPS):
        sib_copy(g).wait_send()
        for copy in far_copies(g):
            copy.wait_send()
        for i in range(2):
            up_copy(g, i).wait_send()
            down_copy(g, i).wait_send()


def per_device(
    gate_signal, key_signal, value_signal, pole_decay, pole_angle, residue_real, residue_imag, skip_gain, out_weight
):
    rows, width = key_signal.shape
    nz = lax.axis_size("ctx") // NX
    quarters = width // LANES
    step = rows // BLOCKS
    group_rows = rows // GROUPS
    outs = out_weight.shape[0] // (2 * NY)
    weight = out_weight.reshape(NY, 2, outs, width)
    f32, bf16 = jnp.float32, jnp.bfloat16
    dma = pltpu.SemaphoreType.DMA

    def vmem(dtype, *shape):
        return pltpu.VMEM(shape, dtype)

    scratch = [
        vmem(bf16, rows, width),
        vmem(bf16, rows, width),
        vmem(bf16, rows, width),
        vmem(f32, MODES, width),
        vmem(f32, MODES, width),
        vmem(f32, MODES, width),
        vmem(f32, MODES, width),
        vmem(f32, 1, width),
        vmem(bf16, NY, outs, width),
        vmem(bf16, NY, outs, width),
        vmem(f32, quarters, 8 * BLOCKS + rows, LANES),
        vmem(f32, quarters, rows, LANES),
        vmem(f32, quarters, step + 1, STATE, LANES),
        vmem(f32, quarters, step, STATE, LANES),
        vmem(f32, quarters, step + 8, LANES),
        vmem(f32, quarters, STATE, LANES),
        vmem(f32, quarters, STATE, LANES),
        vmem(f32, quarters, STATE, LANES),
        vmem(f32, quarters, STATE * BLOCKS, LANES),
        vmem(f32, quarters, STATE, LANES),
        vmem(f32, NX, STATE, LANES),
        vmem(f32, STATE, LANES),
        vmem(f32, nz, STATE, LANES),
        vmem(f32, STATE, LANES),
        vmem(f32, NX, STATE, LANES),
        vmem(f32, NX, STATE, LANES),
        vmem(f32, quarters, STATE * BLOCKS, LANES),
        vmem(f32, quarters, rows, LANES),
        vmem(bf16, rows, width),
        vmem(bf16, rows, width),
        vmem(bf16, GROUPS, group_rows, outs),
        vmem(bf16, GROUPS, group_rows, outs),
        vmem(bf16, GROUPS, group_rows, outs),
        vmem(bf16, GROUPS, group_rows, outs),
        vmem(bf16, GROUPS, group_rows, outs),
        vmem(bf16, GROUPS, group_rows, outs),
        vmem(f32, group_rows // 2, outs),
        vmem(f32, group_rows // 2, outs),
        vmem(f32, rows, outs),
        vmem(f32, outs // LANES, rows, LANES),
        dma((9,)),
        dma((2,)),
        dma((NX,)),
        dma((NX,)),
        dma((nz,)),
        dma((nz,)),
        dma((NX,)),
        dma((NX,)),
        dma((GROUPS,)),
        dma((GROUPS,)),
        dma((GROUPS, 2)),
        dma((GROUPS, 2)),
        dma((GROUPS, 2)),
        dma((GROUPS, 2)),
        dma((GROUPS, 2)),
        dma((GROUPS, 2)),
    ]
    hbm = pl.BlockSpec(memory_space=pl.ANY)
    return pl.pallas_call(
        functools.partial(kernel, nz),
        out_shape=jax.ShapeDtypeStruct((rows, outs), bf16),
        in_specs=[hbm] * 9,
        out_specs=pl.BlockSpec(memory_space=pltpu.VMEM),
        scratch_shapes=scratch,
        compiler_params=pltpu.CompilerParams(
            collective_id=0, has_side_effects=True, vmem_limit_bytes=40 * 1024 * 1024
        ),
    )(
        gate_signal,
        key_signal,
        value_signal,
        pole_decay,
        pole_angle,
        residue_real,
        residue_imag,
        skip_gain.reshape(1, width),
        weight,
    )


def solution(mesh):
    return jax.shard_map(
        per_device,
        mesh=mesh,
        in_specs=(
            P("ctx", "ch"),
            P("ctx", "ch"),
            P("ctx", "ch"),
            P(None, "ch"),
            P(None, "ch"),
            P(None, "ch"),
            P(None, "ch"),
            P("ch"),
            P(None, "ch"),
        ),
        out_specs=P("ctx", "ch"),
        check_vma=False,
    )
```

```python
import functools

import jax
import jax.numpy as jnp
from jax import lax
from jax.experimental import pallas as pl
from jax.experimental.pallas import tpu as pltpu
from jax.sharding import PartitionSpec as P

MESH = pl.DeviceIdType.MESH
MODES = 16
STATE = 2 * MODES
LANES = 128
BLOCKS = 8
NX = 4
NY = 4
GROUP_ROWS = (64, 192)
GROUPS = len(GROUP_ROWS)


def cmul(ar, ai, br, bi):
    return ar * br - ai * bi, ar * bi + ai * br


def advanced(step, state):
    real, imag = cmul(step[:MODES], step[MODES:], state[:MODES], state[MODES:])
    return jnp.concatenate([real, imag], axis=0)


def kernel(
    nz,
    gate,
    key,
    value,
    decay,
    angle,
    res_real,
    res_imag,
    skip,
    weight,
    out,
    gate_v,
    key_v,
    value_v,
    decay_v,
    angle_v,
    real_v,
    imag_v,
    skip_v,
    w_all,
    u,
    g_perm,
    power,
    ker,
    taps,
    lam_block,
    lam_span,
    lam_row,
    sums,
    tot,
    tot_in,
    row_tot,
    row_in,
    before,
    start_out,
    start_in,
    states,
    local,
    g_all,
    far_out,
    far_in,
    up_out,
    up_in,
    down_out,
    down_in,
    up_part,
    down_part,
    own_part,
    final,
    load_sem,
    wsib_sem,
    tot_send,
    tot_recv,
    row_send,
    row_recv,
    start_send,
    start_recv,
    gsib_send,
    gsib_recv,
    far_send,
    far_recv,
    up_send,
    up_recv,
    down_send,
    down_recv,
):
    rows, width = key_v.shape
    step = rows // BLOCKS
    quarters = width // LANES
    ctx, ch = lax.axis_index("ctx"), lax.axis_index("ch")
    z, x = ctx // NX, lax.rem(ctx, NX)
    y, core = ch // 2, lax.rem(ch, 2)
    sibling = {"ctx": ctx, "ch": y * 2 + (1 - core)}
    y_up, y_down, y_far = (lax.rem(y + d, NY) for d in (1, NY - 1, 2))
    up_dev = {"ctx": ctx, "ch": y_up * 2 + core}
    down_dev = {"ctx": ctx, "ch": y_down * 2 + core}

    def remote(src, dst, send, recv, device):
        return pltpu.make_async_remote_copy(
            src_ref=src, dst_ref=dst, send_sem=send, recv_sem=recv, device_id=device, device_id_type=MESH
        )

    pairs = (
        (decay, decay_v),
        (angle, angle_v),
        (key, key_v),
        (value, value_v),
        (res_real, real_v),
        (res_imag, imag_v),
        (skip, skip_v),
        (gate, gate_v),
        (weight.at[:, core], w_all.at[:, :, :width]),
    )
    loads = [pltpu.make_async_copy(src, dst, load_sem.at[i]) for i, (src, dst) in enumerate(pairs)]
    for load in loads:
        load.start()

    barrier = pltpu.get_barrier_semaphore()
    peers = [sibling, up_dev, down_dev]
    peers += [{"ctx": z * NX + lax.rem(x + d, NX), "ch": ch} for d in range(1, NX)]
    peers += [{"ctx": lax.rem(z + d, nz) * NX + x, "ch": ch} for d in range(1, nz)]
    for peer in peers:
        pl.semaphore_signal(barrier, inc=1, device_id=peer, device_id_type=MESH)

    loads[0].wait()
    loads[1].wait()
    magnitude = jnp.exp(-decay_v[...])
    lam_r = magnitude * jnp.cos(angle_v[...])
    lam_i = magnitude * jnp.sin(angle_v[...])

    def lanes(q):
        return slice(q * LANES, (q + 1) * LANES)

    def store_power(j, carry):
        pr, pi = carry
        for q in range(quarters):
            power[q, j, :MODES, :] = pr[:, lanes(q)]
            power[q, j, MODES:, :] = pi[:, lanes(q)]
        return cmul(pr, pi, lam_r, lam_i)

    pr, pi = lax.fori_loop(0, step, store_power, (jnp.ones_like(lam_r), jnp.zeros_like(lam_r)))
    for q in range(quarters):
        power[q, step, :MODES, :] = pr[:, lanes(q)]
        power[q, step, MODES:, :] = pi[:, lanes(q)]
        lam_block[q, :MODES, :] = pr[:, lanes(q)]
        lam_block[q, MODES:, :] = pi[:, lanes(q)]
    for _ in range(3):
        pr, pi = cmul(pr, pi, pr, pi)
    for q in range(quarters):
        lam_span[q, :MODES, :] = pr[:, lanes(q)]
        lam_span[q, MODES:, :] = pi[:, lanes(q)]
    for _ in range(2):
        pr, pi = cmul(pr, pi, pr, pi)
    for q in range(quarters):
        lam_row[q, :MODES, :] = pr[:, lanes(q)]
        lam_row[q, MODES:, :] = pi[:, lanes(q)]

    loads[2].wait()
    loads[3].wait()
    for q in range(quarters):
        u[q, : 8 * BLOCKS, :] = jnp.zeros((8 * BLOCKS, LANES), jnp.float32)
        for b in range(BLOCKS):
            part = slice(b * step, (b + 1) * step)
            drive = key_v[part, lanes(q)].astype(jnp.float32) * value_v[part, lanes(q)].astype(jnp.float32)
            u[q, pl.ds(8 * BLOCKS + b, step, stride=BLOCKS), :] = drive

    w_copy = remote(weight.at[:, 1 - core], w_all.at[:, :, width:], wsib_sem.at[0], wsib_sem.at[1], sibling)

    def total_of(i, _):
        q = lax.rem(x + jnp.where(i == 0, 2, jnp.where(i == 1, 1, jnp.where(i == 2, 3, 0))), NX)

        def add_token(j, acc):
            row = u[q, pl.ds(pl.multiple_of(8 * BLOCKS + j * BLOCKS, BLOCKS), BLOCKS), :]
            return tuple(acc[k] + power[q, step - 1 - j, pl.ds(k, 1), :] * row for k in range(STATE))

        acc = lax.fori_loop(
            0, step, add_token, tuple(jnp.zeros((BLOCKS, LANES), jnp.float32) for _ in range(STATE)), unroll=2
        )
        for k in range(STATE):
            sums[q, pl.ds(k, BLOCKS, stride=STATE), :] = acc[k]
        lam = lam_block[q]
        state = sums[q, :STATE, :]
        for b in range(1, BLOCKS):
            state = advanced(lam, state) + sums[q, b * STATE : (b + 1) * STATE, :]
        tot[q] = state

        @pl.when(i == 0)
        def _():
            pl.semaphore_wait(barrier, len(peers))

        @pl.when(i < NX - 1)
        def _():
            remote(
                tot.at[q], tot_in.at[x], tot_send.at[q], tot_recv.at[x], {"ctx": z * NX + q, "ch": ch}
            ).start()

        @pl.when(i == NX - 1)
        def _():
            tot_in[x] = state

        return 0

    lax.fori_loop(0, quarters, total_of, 0)
    w_copy.start()

    for i in (4, 5, 6):
        loads[i].wait()
    for q in range(quarters):
        rr, ri = real_v[:, lanes(q)], imag_v[:, lanes(q)]
        taps[q, 0:1, :] = jnp.sum(rr, axis=0, keepdims=True) + skip_v[:, lanes(q)]

        def store_ker(j, _, q=q, rr=rr, ri=ri):
            p = power[q, j + 1]
            kr, ki = cmul(rr, ri, p[:MODES], p[MODES:])
            ker[q, j, :MODES, :] = kr
            ker[q, j, MODES:, :] = -ki
            taps[q, pl.ds(j + 1, 1), :] = jnp.sum(kr, axis=0, keepdims=True)
            return 0

        lax.fori_loop(0, step, store_ker, 0, unroll=4)

    for d in range(1, NX):
        src = lax.rem(x + d, NX)
        remote(tot.at[src], tot_in.at[src], tot_send.at[src], tot_recv.at[src], sibling).wait_recv()
    lam = lam_span[x]
    state = tot_in[0]
    for i in range(1, NX):
        state = advanced(lam, state) + tot_in[i]
    row_tot[...] = state

    def row_copy(d):
        return remote(
            row_tot, row_in.at[z], row_send.at[d], row_recv.at[z], {"ctx": lax.rem(z + d, nz) * NX + x, "ch": ch}
        )

    for d in reversed(range(1, nz)):

        @pl.when(z + d < nz)
        def _():
            row_copy(d).start()

    loads[7].wait()
    chunk = 8 * BLOCKS

    def fir(q, _):
        for c in range(step // 8):
            acc = None
            for lag in range(8 * c + 8):
                begin = chunk + c * chunk - lag * BLOCKS
                term = taps[q, pl.ds(lag, 1), :] * u[q, begin : begin + chunk, :]
                acc = term if acc is None else acc + term
            local[q, c * chunk : (c + 1) * chunk, :] = acc
        return 0

    lax.fori_loop(0, quarters, fir, 0)
    for q in range(quarters):
        for b in range(BLOCKS):
            part = slice(b * step, (b + 1) * step)
            g_perm[q, pl.ds(b, step, stride=BLOCKS), :] = gate_v[part, lanes(q)].astype(jnp.float32)

    lam = lam_row[x]
    before[...] = jnp.zeros_like(before)
    for s in range(nz - 1):

        @pl.when(s < z)
        def _():
            remote(row_tot, row_in.at[s], row_send.at[0], row_recv.at[s], sibling).wait_recv()
            before[...] = advanced(lam, before[...]) + row_in[s]

    lam = lam_span[x]
    state = before[...]
    for i in range(NX):
        start_out[i] = state
        if i < NX - 1:
            state = advanced(lam, state) + tot_in[i]
    for d in (2, 1, 3):
        to = lax.rem(x + d, NX)
        remote(
            start_out.at[to], start_in.at[x], start_send.at[d], start_recv.at[x], {"ctx": z * NX + to, "ch": ch}
        ).start()
    start_in[x] = start_out[x]
    for d in range(1, NX):
        src = lax.rem(x + d, NX)
        remote(start_out.at[src], start_in.at[src], start_send.at[0], start_recv.at[src], sibling).wait_recv()

    for q in range(quarters):
        lam = lam_block[q]
        state = start_in[q]
        for b in range(BLOCKS):
            states[q, pl.ds(b, STATE, stride=BLOCKS), :] = state
            if b < BLOCKS - 1:
                state = advanced(lam, state) + sums[q, b * STATE : (b + 1) * STATE, :]

    def rows_of(g):
        begin = sum(GROUP_ROWS[:g])
        return slice(begin, begin + GROUP_ROWS[g])

    def halves_of(g):
        at = rows_of(g)
        middle = (at.start + at.stop) // 2
        return slice(at.start, middle), slice(middle, at.stop)

    def gated(g):
        at_rows = rows_of(g)

        for q in range(quarters):
            held = [states[q, k * BLOCKS : (k + 1) * BLOCKS, :] for k in range(STATE)]

            def two_tokens(i, _, q=q, held=held):
                done = []
                for t in range(2):
                    j = 2 * i + t
                    at = pl.ds(pl.multiple_of(j * BLOCKS, BLOCKS), BLOCKS)
                    partial = [local[q, at, :], None, None, None]
                    for k in range(STATE):
                        term = ker[q, j, pl.ds(k, 1), :] * held[k]
                        partial[k % 4] = term if partial[k % 4] is None else partial[k % 4] + term
                    total = (partial[0] + partial[1]) + (partial[2] + partial[3])
                    done.append(total * g_perm[q, at, :])
                to = pl.ds(pl.multiple_of(i * 2 * BLOCKS, 2 * BLOCKS), 2 * BLOCKS)
                g_all[to, lanes(q)] = jnp.concatenate(done, axis=0).astype(jnp.bfloat16)
                return 0

            lax.fori_loop(at_rows.start // (2 * BLOCKS), at_rows.stop // (2 * BLOCKS), two_tokens, 0)

    def sib_copy(g):
        at = rows_of(g)
        return remote(g_all.at[at, :width], g_all.at[at, width:], gsib_send.at[g], gsib_recv.at[g], sibling)

    def product(g, to):
        return lax.dot_general(
            g_all[rows_of(g), :], w_all[to], (((1,), (1,)), ((), ())), preferred_element_type=jnp.float32
        )

    def far_copies(g):
        low, high = halves_of(g)
        return (
            remote(far_out.at[low], far_in.at[low], far_send.at[g, 0], far_recv.at[g, 0], up_dev),
            remote(far_out.at[high], far_in.at[high], far_send.at[g, 1], far_recv.at[g, 1], down_dev),
        )

    def up_copy(g, i):
        at = halves_of(g)[i]
        return remote(up_out.at[at], up_in.at[at], up_send.at[g, i], up_recv.at[g, i], up_dev)

    def down_copy(g, i):
        at = halves_of(g)[i]
        return remote(down_out.at[at], down_in.at[at], down_send.at[g, i], down_recv.at[g, i], down_dev)

    def send_off(g):
        low, high = halves_of(g)
        half = GROUP_ROWS[g] // 2
        far_out[rows_of(g), :] = product(g, y_far).astype(jnp.bfloat16)
        for copy in far_copies(g):
            copy.start()
        part = product(g, y_up)
        up_out[high, :] = part[half:].astype(jnp.bfloat16)
        up_copy(g, 1).start()
        up_part[low, :] = part[:half]
        part = product(g, y_down)
        down_out[low, :] = part[:half].astype(jnp.bfloat16)
        down_copy(g, 0).start()
        down_part[high, :] = part[half:]

    def send_rest(g):
        low, high = halves_of(g)
        arrived = far_copies(g)
        arrived[0].wait_recv()
        up_out[low, :] = (up_part[low, :] + far_in[low, :].astype(jnp.float32)).astype(jnp.bfloat16)
        up_copy(g, 0).start()
        arrived[1].wait_recv()
        down_out[high, :] = (down_part[high, :] + far_in[high, :].astype(jnp.float32)).astype(jnp.bfloat16)
        down_copy(g, 1).start()
        own_part[rows_of(g), :] = product(g, y)

    for g in range(GROUPS + 1):
        if g < GROUPS:
            gated(g)
            sib_copy(g).start()
        if g == 0:
            loads[8].wait()
            w_copy.wait_recv()
        if g > 0:
            sib_copy(g - 1).wait_recv()
            send_off(g - 1)
        if g > 1:
            send_rest(g - 2)
    send_rest(GROUPS - 1)

    for g in range(GROUPS):
        for i in (1, 0):
            down_copy(g, 1 - i).wait_recv()
            up_copy(g, i).wait_recv()
        at = rows_of(g)
        whole = own_part[at, :] + up_in[at, :].astype(jnp.float32) + down_in[at, :].astype(jnp.float32)
        for q in range(quarters):
            final[q, at, :] = whole[:, lanes(q)]
    for q in range(quarters):
        for b in range(BLOCKS):
            out[b * step : (b + 1) * step, lanes(q)] = final[q, pl.ds(b, step, stride=BLOCKS), :].astype(jnp.bfloat16)

    w_copy.wait_send()
    for d in range(1, NX):
        q = lax.rem(x + d, NX)
        remote(tot.at[q], tot_in.at[x], tot_send.at[q], tot_recv.at[x], sibling).wait_send()
        remote(start_out.at[q], start_in.at[x], start_send.at[d], start_recv.at[x], sibling).wait_send()
    for d in range(1, nz):

        @pl.when(z + d < nz)
        def _():
            row_copy(d).wait_send()

    for g in range(GROUPS):
        sib_copy(g).wait_send()
        for copy in far_copies(g):
            copy.wait_send()
        for i in range(2):
            up_copy(g, i).wait_send()
            down_copy(g, i).wait_send()


def per_device(
    gate_signal, key_signal, value_signal, pole_decay, pole_angle, residue_real, residue_imag, skip_gain, out_weight
):
    rows, width = key_signal.shape
    nz = lax.axis_size("ctx") // NX
    quarters = width // LANES
    step = rows // BLOCKS
    outs = out_weight.shape[0] // (2 * NY)
    weight = out_weight.reshape(NY, 2, outs, width)
    f32, bf16 = jnp.float32, jnp.bfloat16
    dma = pltpu.SemaphoreType.DMA

    def vmem(dtype, *shape):
        return pltpu.VMEM(shape, dtype)

    scratch = [
        vmem(bf16, rows, width),
        vmem(bf16, rows, width),
        vmem(bf16, rows, width),
        vmem(f32, MODES, width),
        vmem(f32, MODES, width),
        vmem(f32, MODES, width),
        vmem(f32, MODES, width),
        vmem(f32, 1, width),
        vmem(bf16, NY, outs, 2 * width),
        vmem(f32, quarters, 8 * BLOCKS + rows, LANES),
        vmem(f32, quarters, rows, LANES),
        vmem(f32, quarters, step + 1, STATE, LANES),
        vmem(f32, quarters, step, STATE, LANES),
        vmem(f32, quarters, step + 8, LANES),
        vmem(f32, quarters, STATE, LANES),
        vmem(f32, quarters, STATE, LANES),
        vmem(f32, quarters, STATE, LANES),
        vmem(f32, quarters, STATE * BLOCKS, LANES),
        vmem(f32, quarters, STATE, LANES),
        vmem(f32, NX, STATE, LANES),
        vmem(f32, STATE, LANES),
        vmem(f32, nz, STATE, LANES),
        vmem(f32, STATE, LANES),
        vmem(f32, NX, STATE, LANES),
        vmem(f32, NX, STATE, LANES),
        vmem(f32, quarters, STATE * BLOCKS, LANES),
        vmem(f32, quarters, rows, LANES),
        vmem(bf16, rows, 2 * width),
        vmem(bf16, rows, outs),
        vmem(bf16, rows, outs),
        vmem(bf16, rows, outs),
        vmem(bf16, rows, outs),
        vmem(bf16, rows, outs),
        vmem(bf16, rows, outs),
        vmem(f32, rows, outs),
        vmem(f32, rows, outs),
        vmem(f32, rows, outs),
        vmem(f32, outs // LANES, rows, LANES),
        dma((9,)),
        dma((2,)),
        dma((NX,)),
        dma((NX,)),
        dma((nz,)),
        dma((nz,)),
        dma((NX,)),
        dma((NX,)),
        dma((GROUPS,)),
        dma((GROUPS,)),
        dma((GROUPS, 2)),
        dma((GROUPS, 2)),
        dma((GROUPS, 2)),
        dma((GROUPS, 2)),
        dma((GROUPS, 2)),
        dma((GROUPS, 2)),
    ]
    hbm = pl.BlockSpec(memory_space=pltpu.HBM)
    return pl.pallas_call(
        functools.partial(kernel, nz),
        out_shape=jax.ShapeDtypeStruct((rows, outs), bf16),
        in_specs=[hbm] * 9,
        out_specs=pl.BlockSpec(memory_space=pltpu.VMEM),
        scratch_shapes=scratch,
        compiler_params=pltpu.CompilerParams(
            collective_id=0, has_side_effects=True, vmem_limit_bytes=48 * 1024 * 1024
        ),
    )(
        *(
            pltpu.with_memory_space_constraint(array, pltpu.HBM)
            for array in (
                gate_signal,
                key_signal,
                value_signal,
                pole_decay,
                pole_angle,
                residue_real,
                residue_imag,
                skip_gain.reshape(1, width),
                weight,
            )
        )
    )


def solution(mesh):
    return jax.shard_map(
        per_device,
        mesh=mesh,
        in_specs=(
            P("ctx", "ch"),
            P("ctx", "ch"),
            P("ctx", "ch"),
            P(None, "ch"),
            P(None, "ch"),
            P(None, "ch"),
            P(None, "ch"),
            P("ch"),
            P(None, "ch"),
        ),
        out_specs=P("ctx", "ch"),
        check_vma=False,
    )
```

```python
import functools

import jax
import jax.numpy as jnp
from jax import lax
from jax.experimental import pallas as pl
from jax.experimental.pallas import tpu as pltpu
from jax.sharding import PartitionSpec as P

MESH = pl.DeviceIdType.MESH
MODES = 16
STATE = 2 * MODES
LANES = 128
BLOCKS = 8
NX = 4
NY = 4
GROUP_ROWS = (64, 64, 128)
GROUPS = len(GROUP_ROWS)


def cmul(ar, ai, br, bi):
    return ar * br - ai * bi, ar * bi + ai * br


def advanced(step, state):
    real, imag = cmul(step[:MODES], step[MODES:], state[:MODES], state[MODES:])
    return jnp.concatenate([real, imag], axis=0)


def kernel(
    nz,
    gate,
    key,
    value,
    decay,
    angle,
    res_real,
    res_imag,
    skip,
    weight,
    out,
    gate_v,
    key_v,
    value_v,
    decay_v,
    angle_v,
    real_v,
    imag_v,
    skip_v,
    w_all,
    w_t,
    u,
    g_perm,
    power,
    ker,
    taps,
    lam_block,
    lam_span,
    lam_row,
    sums,
    tot,
    tot_in,
    row_tot,
    row_in,
    before,
    start_out,
    start_in,
    states,
    local,
    g_all,
    far_out,
    far_in,
    up_out,
    up_in,
    down_out,
    down_in,
    up_part,
    down_part,
    own_part,
    final,
    load_sem,
    wsib_sem,
    tot_send,
    tot_recv,
    row_send,
    row_recv,
    start_send,
    start_recv,
    gsib_send,
    gsib_recv,
    far_send,
    far_recv,
    up_send,
    up_recv,
    down_send,
    down_recv,
    ready,
):
    rows, width = key_v.shape
    step = rows // BLOCKS
    quarters = width // LANES
    ctx, ch = lax.axis_index("ctx"), lax.axis_index("ch")
    z, x = ctx // NX, lax.rem(ctx, NX)
    y, core = ch // 2, lax.rem(ch, 2)
    sibling = {"ctx": ctx, "ch": y * 2 + (1 - core)}
    y_up, y_down, y_far = (lax.rem(y + d, NY) for d in (1, NY - 1, 2))
    up_dev = {"ctx": ctx, "ch": y_up * 2 + core}
    down_dev = {"ctx": ctx, "ch": y_down * 2 + core}

    def remote(src, dst, send, recv, device):
        return pltpu.make_async_remote_copy(
            src_ref=src, dst_ref=dst, send_sem=send, recv_sem=recv, device_id=device, device_id_type=MESH
        )

    pairs = (
        (decay, decay_v),
        (angle, angle_v),
        (key, key_v),
        (value, value_v),
        (res_real, real_v),
        (res_imag, imag_v),
        (skip, skip_v),
        (gate, gate_v),
        (weight.at[:, core], w_all.at[:, :, :width]),
    )
    loads = [pltpu.make_async_copy(src, dst, load_sem.at[i]) for i, (src, dst) in enumerate(pairs)]
    for load in loads:
        load.start()

    barrier = pltpu.get_barrier_semaphore()
    peers = [sibling, up_dev, down_dev]
    peers += [{"ctx": z * NX + lax.rem(x + d, NX), "ch": ch} for d in range(1, NX)]
    for peer in peers:
        pl.semaphore_signal(barrier, inc=1, device_id=peer, device_id_type=MESH)
    for d in range(1, nz):

        @pl.when(z + d < nz)
        def _():
            later = {"ctx": (z + d) * NX + x, "ch": ch}
            pl.semaphore_signal(barrier, inc=1, device_id=later, device_id_type=MESH)

    pl.semaphore_wait(barrier, len(peers) + z)
    for d in range(1, nz):

        @pl.when(z >= d)
        def _():
            earlier = {"ctx": (z - d) * NX + x, "ch": ch}
            pl.semaphore_signal(ready.at[d], inc=1, device_id=earlier, device_id_type=MESH)

    w_copy = remote(weight.at[:, 1 - core], w_all.at[:, :, width:], wsib_sem.at[0], wsib_sem.at[1], sibling)
    w_copy.start()

    loads[0].wait()
    loads[1].wait()
    magnitude = jnp.exp(-decay_v[...])
    lam_r = magnitude * jnp.cos(angle_v[...])
    lam_i = magnitude * jnp.sin(angle_v[...])

    def lanes(q):
        return slice(q * LANES, (q + 1) * LANES)

    def store_power(j, carry):
        pr, pi = carry
        for q in range(quarters):
            power[q, j, :MODES, :] = pr[:, lanes(q)]
            power[q, j, MODES:, :] = pi[:, lanes(q)]
        return cmul(pr, pi, lam_r, lam_i)

    pr, pi = lax.fori_loop(0, step, store_power, (jnp.ones_like(lam_r), jnp.zeros_like(lam_r)))
    for q in range(quarters):
        power[q, step, :MODES, :] = pr[:, lanes(q)]
        power[q, step, MODES:, :] = pi[:, lanes(q)]
        lam_block[q, :MODES, :] = pr[:, lanes(q)]
        lam_block[q, MODES:, :] = pi[:, lanes(q)]
    for _ in range(3):
        pr, pi = cmul(pr, pi, pr, pi)
    for q in range(quarters):
        lam_span[q, :MODES, :] = pr[:, lanes(q)]
        lam_span[q, MODES:, :] = pi[:, lanes(q)]
    for _ in range(2):
        pr, pi = cmul(pr, pi, pr, pi)
    for q in range(quarters):
        lam_row[q, :MODES, :] = pr[:, lanes(q)]
        lam_row[q, MODES:, :] = pi[:, lanes(q)]

    loads[2].wait()
    loads[3].wait()
    for q in range(quarters):
        u[q, : 8 * BLOCKS, :] = jnp.zeros((8 * BLOCKS, LANES), jnp.float32)
        for b in range(BLOCKS):
            part = slice(b * step, (b + 1) * step)
            drive = key_v[part, lanes(q)].astype(jnp.float32) * value_v[part, lanes(q)].astype(jnp.float32)
            u[q, pl.ds(8 * BLOCKS + b, step, stride=BLOCKS), :] = drive


    def total_of(i, _):
        q = lax.rem(x + jnp.where(i == 0, 2, jnp.where(i == 1, 1, jnp.where(i == 2, 3, 0))), NX)

        def add_token(j, acc):
            row = u[q, pl.ds(pl.multiple_of(8 * BLOCKS + j * BLOCKS, BLOCKS), BLOCKS), :]
            return tuple(acc[k] + power[q, step - 1 - j, pl.ds(k, 1), :] * row for k in range(STATE))

        acc = lax.fori_loop(
            0, step, add_token, tuple(jnp.zeros((BLOCKS, LANES), jnp.float32) for _ in range(STATE)), unroll=8
        )
        for k in range(STATE):
            sums[q, pl.ds(k, BLOCKS, stride=STATE), :] = acc[k]
        lam = lam_block[q]
        state = sums[q, :STATE, :]
        for b in range(1, BLOCKS):
            state = advanced(lam, state) + sums[q, b * STATE : (b + 1) * STATE, :]
        tot[q] = state

        @pl.when(i < NX - 1)
        def _():
            remote(
                tot.at[q], tot_in.at[x], tot_send.at[q], tot_recv.at[x], {"ctx": z * NX + q, "ch": ch}
            ).start()

        @pl.when(i == NX - 1)
        def _():
            tot_in[x] = state

        return 0

    lax.fori_loop(0, quarters, total_of, 0)

    for i in (4, 5, 6):
        loads[i].wait()
    for q in range(quarters):
        rr, ri = real_v[:, lanes(q)], imag_v[:, lanes(q)]
        taps[q, 0:1, :] = jnp.sum(rr, axis=0, keepdims=True) + skip_v[:, lanes(q)]

        def store_ker(j, _, q=q, rr=rr, ri=ri):
            p = power[q, j + 1]
            kr, ki = cmul(rr, ri, p[:MODES], p[MODES:])
            ker[q, j, :MODES, :] = kr
            ker[q, j, MODES:, :] = -ki
            taps[q, pl.ds(j + 1, 1), :] = jnp.sum(kr, axis=0, keepdims=True)
            return 0

        lax.fori_loop(0, step, store_ker, 0, unroll=4)

    for d in range(1, NX):
        src = lax.rem(x + d, NX)
        remote(tot.at[src], tot_in.at[src], tot_send.at[src], tot_recv.at[src], sibling).wait_recv()
    lam = lam_span[x]
    state = tot_in[0]
    for i in range(1, NX):
        state = advanced(lam, state) + tot_in[i]
    row_tot[...] = state

    def row_copy(d):
        return remote(
            row_tot, row_in.at[z], row_send.at[d], row_recv.at[z], {"ctx": lax.rem(z + d, nz) * NX + x, "ch": ch}
        )

    def send_row(d):
        @pl.when(z + d < nz)
        def _():
            pl.semaphore_wait(ready.at[d], 1)
            row_copy(d).start()

    by_distance = sorted(range(1, nz), key=lambda d: (min(d, nz - d), d))
    for d in by_distance[:-1]:
        send_row(d)

    loads[7].wait()
    chunk = 8 * BLOCKS

    def fir(q, _):
        for c in range(step // 8):
            acc = None
            for lag in range(8 * c + 8):
                begin = chunk + c * chunk - lag * BLOCKS
                term = taps[q, pl.ds(lag, 1), :] * u[q, begin : begin + chunk, :]
                acc = term if acc is None else acc + term
            local[q, c * chunk : (c + 1) * chunk, :] = acc
        return 0

    lax.fori_loop(0, quarters, fir, 0)
    for q in range(quarters):
        for b in range(BLOCKS):
            part = slice(b * step, (b + 1) * step)
            g_perm[q, pl.ds(b, step, stride=BLOCKS), :] = gate_v[part, lanes(q)].astype(jnp.float32)

    send_row(by_distance[-1])

    lam = lam_row[x]
    before[...] = jnp.zeros_like(before)
    for s in range(nz - 1):

        @pl.when(s < z)
        def _():
            remote(row_tot, row_in.at[s], row_send.at[0], row_recv.at[s], sibling).wait_recv()
            before[...] = advanced(lam, before[...]) + row_in[s]

    lam = lam_span[x]
    state = before[...]
    for i in range(NX):
        start_out[i] = state
        if i < NX - 1:
            state = advanced(lam, state) + tot_in[i]
    for d in (2, 1, 3):
        to = lax.rem(x + d, NX)
        remote(
            start_out.at[to], start_in.at[x], start_send.at[d], start_recv.at[x], {"ctx": z * NX + to, "ch": ch}
        ).start()
    start_in[x] = start_out[x]

    loads[8].wait()
    for to in range(NY):
        w_t[to, :width, :] = w_all[to, :, :width].T
    w_copy.wait_recv()
    for to in range(NY):
        w_t[to, width:, :] = w_all[to, :, width:].T

    for d in range(1, NX):
        src = lax.rem(x + d, NX)
        remote(start_out.at[src], start_in.at[src], start_send.at[0], start_recv.at[src], sibling).wait_recv()

    for q in range(quarters):
        lam = lam_block[q]
        state = start_in[q]
        for b in range(BLOCKS):
            states[q, pl.ds(b, STATE, stride=BLOCKS), :] = state
            if b < BLOCKS - 1:
                state = advanced(lam, state) + sums[q, b * STATE : (b + 1) * STATE, :]

    def rows_of(g):
        begin = sum(GROUP_ROWS[:g])
        return slice(begin, begin + GROUP_ROWS[g])

    def halves_of(g):
        at = rows_of(g)
        middle = (at.start + at.stop) // 2
        return slice(at.start, middle), slice(middle, at.stop)

    def gated(g):
        at_rows = rows_of(g)

        for q in range(quarters):
            held = [states[q, k * BLOCKS : (k + 1) * BLOCKS, :] for k in range(STATE)]

            def two_tokens(i, _, q=q, held=held):
                done = []
                for t in range(2):
                    j = 2 * i + t
                    at = pl.ds(pl.multiple_of(j * BLOCKS, BLOCKS), BLOCKS)
                    partial = [local[q, at, :], None, None, None]
                    for k in range(STATE):
                        term = ker[q, j, pl.ds(k, 1), :] * held[k]
                        partial[k % 4] = term if partial[k % 4] is None else partial[k % 4] + term
                    total = (partial[0] + partial[1]) + (partial[2] + partial[3])
                    done.append(total * g_perm[q, at, :])
                to = pl.ds(pl.multiple_of(i * 2 * BLOCKS, 2 * BLOCKS), 2 * BLOCKS)
                g_all[to, lanes(q)] = jnp.concatenate(done, axis=0).astype(jnp.bfloat16)
                return 0

            lax.fori_loop(at_rows.start // (2 * BLOCKS), at_rows.stop // (2 * BLOCKS), two_tokens, 0, unroll=4)

    def sib_copy(g):
        at = rows_of(g)
        return remote(g_all.at[at, :width], g_all.at[at, width:], gsib_send.at[g], gsib_recv.at[g], sibling)

    def product(g, to):
        return lax.dot_general(
            g_all[rows_of(g), :], w_t[to], (((1,), (0,)), ((), ())), preferred_element_type=jnp.float32
        )

    def far_copies(g):
        low, high = halves_of(g)
        return (
            remote(far_out.at[low], far_in.at[low], far_send.at[g, 0], far_recv.at[g, 0], up_dev),
            remote(far_out.at[high], far_in.at[high], far_send.at[g, 1], far_recv.at[g, 1], down_dev),
        )

    def up_copy(g, i):
        at = halves_of(g)[i]
        return remote(up_out.at[at], up_in.at[at], up_send.at[g, i], up_recv.at[g, i], up_dev)

    def down_copy(g, i):
        at = halves_of(g)[i]
        return remote(down_out.at[at], down_in.at[at], down_send.at[g, i], down_recv.at[g, i], down_dev)

    def send_off(g):
        low, high = halves_of(g)
        half = GROUP_ROWS[g] // 2
        far_out[rows_of(g), :] = product(g, y_far).astype(jnp.bfloat16)
        for copy in far_copies(g):
            copy.start()
        part = product(g, y_up)
        up_out[high, :] = part[half:].astype(jnp.bfloat16)
        up_copy(g, 1).start()
        up_part[low, :] = part[:half]
        part = product(g, y_down)
        down_out[low, :] = part[:half].astype(jnp.bfloat16)
        down_copy(g, 0).start()
        down_part[high, :] = part[half:]

    def send_rest(g):
        low, high = halves_of(g)
        arrived = far_copies(g)
        arrived[0].wait_recv()
        up_out[low, :] = (up_part[low, :] + far_in[low, :].astype(jnp.float32)).astype(jnp.bfloat16)
        up_copy(g, 0).start()
        arrived[1].wait_recv()
        down_out[high, :] = (down_part[high, :] + far_in[high, :].astype(jnp.float32)).astype(jnp.bfloat16)
        down_copy(g, 1).start()

    def keep_own(g):
        own_part[rows_of(g), :] = product(g, y)

    for g in range(2):
        gated(g)
        sib_copy(g).start()
    for g in range(2):
        sib_copy(g).wait_recv()
        send_off(g)
    gated(2)
    sib_copy(2).start()
    send_rest(0)
    keep_own(0)
    sib_copy(2).wait_recv()
    send_off(2)
    send_rest(1)
    send_rest(2)
    keep_own(1)
    keep_own(2)

    for g in range(GROUPS):
        for i in (1, 0):
            down_copy(g, 1 - i).wait_recv()
            up_copy(g, i).wait_recv()
        at = rows_of(g)
        whole = own_part[at, :] + up_in[at, :].astype(jnp.float32) + down_in[at, :].astype(jnp.float32)
        for q in range(quarters):
            final[q, at, :] = whole[:, lanes(q)]
    for q in range(quarters):
        for b in range(BLOCKS):
            out[b * step : (b + 1) * step, lanes(q)] = final[q, pl.ds(b, step, stride=BLOCKS), :].astype(jnp.bfloat16)

    w_copy.wait_send()
    for d in range(1, NX):
        q = lax.rem(x + d, NX)
        remote(tot.at[q], tot_in.at[x], tot_send.at[q], tot_recv.at[x], sibling).wait_send()
        remote(start_out.at[q], start_in.at[x], start_send.at[d], start_recv.at[x], sibling).wait_send()
    for d in range(1, nz):

        @pl.when(z + d < nz)
        def _():
            row_copy(d).wait_send()

    for g in range(GROUPS):
        sib_copy(g).wait_send()
        for copy in far_copies(g):
            copy.wait_send()
        for i in range(2):
            up_copy(g, i).wait_send()
            down_copy(g, i).wait_send()


def per_device(
    gate_signal, key_signal, value_signal, pole_decay, pole_angle, residue_real, residue_imag, skip_gain, out_weight
):
    rows, width = key_signal.shape
    nz = lax.axis_size("ctx") // NX
    quarters = width // LANES
    step = rows // BLOCKS
    outs = out_weight.shape[0] // (2 * NY)
    weight = out_weight.reshape(NY, 2, outs, width)
    f32, bf16 = jnp.float32, jnp.bfloat16
    dma = pltpu.SemaphoreType.DMA

    def vmem(dtype, *shape):
        return pltpu.VMEM(shape, dtype)

    scratch = [
        vmem(bf16, rows, width),
        vmem(bf16, rows, width),
        vmem(bf16, rows, width),
        vmem(f32, MODES, width),
        vmem(f32, MODES, width),
        vmem(f32, MODES, width),
        vmem(f32, MODES, width),
        vmem(f32, 1, width),
        vmem(bf16, NY, outs, 2 * width),
        vmem(bf16, NY, 2 * width, outs),
        vmem(f32, quarters, 8 * BLOCKS + rows, LANES),
        vmem(f32, quarters, rows, LANES),
        vmem(f32, quarters, step + 1, STATE, LANES),
        vmem(f32, quarters, step, STATE, LANES),
        vmem(f32, quarters, step + 8, LANES),
        vmem(f32, quarters, STATE, LANES),
        vmem(f32, quarters, STATE, LANES),
        vmem(f32, quarters, STATE, LANES),
        vmem(f32, quarters, STATE * BLOCKS, LANES),
        vmem(f32, quarters, STATE, LANES),
        vmem(f32, NX, STATE, LANES),
        vmem(f32, STATE, LANES),
        vmem(f32, nz, STATE, LANES),
        vmem(f32, STATE, LANES),
        vmem(f32, NX, STATE, LANES),
        vmem(f32, NX, STATE, LANES),
        vmem(f32, quarters, STATE * BLOCKS, LANES),
        vmem(f32, quarters, rows, LANES),
        vmem(bf16, rows, 2 * width),
        vmem(bf16, rows, outs),
        vmem(bf16, rows, outs),
        vmem(bf16, rows, outs),
        vmem(bf16, rows, outs),
        vmem(bf16, rows, outs),
        vmem(bf16, rows, outs),
        vmem(f32, rows, outs),
        vmem(f32, rows, outs),
        vmem(f32, rows, outs),
        vmem(f32, outs // LANES, rows, LANES),
        dma((9,)),
        dma((2,)),
        dma((NX,)),
        dma((NX,)),
        dma((nz,)),
        dma((nz,)),
        dma((NX,)),
        dma((NX,)),
        dma((GROUPS,)),
        dma((GROUPS,)),
        dma((GROUPS, 2)),
        dma((GROUPS, 2)),
        dma((GROUPS, 2)),
        dma((GROUPS, 2)),
        dma((GROUPS, 2)),
        dma((GROUPS, 2)),
        pltpu.SemaphoreType.REGULAR((nz,)),
    ]
    hbm = pl.BlockSpec(memory_space=pltpu.HBM)
    return pl.pallas_call(
        functools.partial(kernel, nz),
        out_shape=jax.ShapeDtypeStruct((rows, outs), bf16),
        in_specs=[hbm] * 9,
        out_specs=pl.BlockSpec(memory_space=pltpu.VMEM),
        scratch_shapes=scratch,
        compiler_params=pltpu.CompilerParams(
            collective_id=0, has_side_effects=True, vmem_limit_bytes=48 * 1024 * 1024
        ),
    )(
        *(
            pltpu.with_memory_space_constraint(array, pltpu.HBM)
            for array in (
                gate_signal,
                key_signal,
                value_signal,
                pole_decay,
                pole_angle,
                residue_real,
                residue_imag,
                skip_gain.reshape(1, width),
                weight,
            )
        )
    )


def solution(mesh):
    return jax.shard_map(
        per_device,
        mesh=mesh,
        in_specs=(
            P("ctx", "ch"),
            P("ctx", "ch"),
            P("ctx", "ch"),
            P(None, "ch"),
            P(None, "ch"),
            P(None, "ch"),
            P(None, "ch"),
            P("ch"),
            P(None, "ch"),
        ),
        out_specs=P("ctx", "ch"),
        check_vma=False,
    )
```

```python
import functools

import jax
import jax.numpy as jnp
from jax import lax
from jax.experimental import pallas as pl
from jax.experimental.pallas import tpu as pltpu
from jax.sharding import PartitionSpec as P

MESH = pl.DeviceIdType.MESH
MODES = 16
STATE = 2 * MODES
LANES = 128
BLOCKS = 8
NX = 4
NY = 4
GROUP_ROWS = (64, 64, 128)
EARLY = 1
GROUPS = len(GROUP_ROWS)


def cmul(ar, ai, br, bi):
    return ar * br - ai * bi, ar * bi + ai * br


def advanced(step, state):
    real, imag = cmul(step[:MODES], step[MODES:], state[:MODES], state[MODES:])
    return jnp.concatenate([real, imag], axis=0)


def kernel(
    nz,
    gate,
    key,
    value,
    decay,
    angle,
    res_real,
    res_imag,
    skip,
    weight,
    out,
    gate_v,
    key_v,
    value_v,
    decay_v,
    angle_v,
    real_v,
    imag_v,
    skip_v,
    w_all,
    w_t,
    u,
    g_perm,
    power,
    ker,
    taps,
    lam_block,
    lam_span,
    lam_row,
    sums,
    tot,
    tot_in,
    row_tot,
    row_in,
    before,
    start_out,
    start_in,
    states,
    local,
    g_all,
    far_out,
    far_in,
    up_out,
    up_in,
    down_out,
    down_in,
    up_part,
    down_part,
    own_part,
    final,
    load_sem,
    wsib_sem,
    tot_send,
    tot_recv,
    row_send,
    row_recv,
    start_send,
    start_recv,
    gsib_send,
    gsib_recv,
    far_send,
    far_recv,
    up_send,
    up_recv,
    down_send,
    down_recv,
    ready,
):
    rows, width = key_v.shape
    step = rows // BLOCKS
    quarters = width // LANES
    ctx, ch = lax.axis_index("ctx"), lax.axis_index("ch")
    z, x = ctx // NX, lax.rem(ctx, NX)
    y, core = ch // 2, lax.rem(ch, 2)
    sibling = {"ctx": ctx, "ch": y * 2 + (1 - core)}
    y_up, y_down, y_far = (lax.rem(y + d, NY) for d in (1, NY - 1, 2))
    up_dev = {"ctx": ctx, "ch": y_up * 2 + core}
    down_dev = {"ctx": ctx, "ch": y_down * 2 + core}

    def remote(src, dst, send, recv, device):
        return pltpu.make_async_remote_copy(
            src_ref=src, dst_ref=dst, send_sem=send, recv_sem=recv, device_id=device, device_id_type=MESH
        )

    pairs = (
        (decay, decay_v),
        (angle, angle_v),
        (key, key_v),
        (value, value_v),
        (res_real, real_v),
        (res_imag, imag_v),
        (skip, skip_v),
        (gate, gate_v),
        (weight.at[:, core], w_all.at[:, :, :width]),
    )
    loads = [pltpu.make_async_copy(src, dst, load_sem.at[i]) for i, (src, dst) in enumerate(pairs)]
    for load in loads:
        load.start()

    barrier = pltpu.get_barrier_semaphore()
    peers = [sibling, up_dev, down_dev]
    peers += [{"ctx": z * NX + lax.rem(x + d, NX), "ch": ch} for d in range(1, NX)]
    for peer in peers:
        pl.semaphore_signal(barrier, inc=1, device_id=peer, device_id_type=MESH)
    for d in range(1, nz):

        @pl.when(z + d < nz)
        def _():
            later = {"ctx": (z + d) * NX + x, "ch": ch}
            pl.semaphore_signal(barrier, inc=1, device_id=later, device_id_type=MESH)

    pl.semaphore_wait(barrier, len(peers) + z)
    for d in range(1, nz):

        @pl.when(z >= d)
        def _():
            earlier = {"ctx": (z - d) * NX + x, "ch": ch}
            pl.semaphore_signal(ready.at[d], inc=1, device_id=earlier, device_id_type=MESH)

    w_copy = remote(weight.at[:, 1 - core], w_all.at[:, :, width:], wsib_sem.at[0], wsib_sem.at[1], sibling)
    w_copy.start()

    loads[0].wait()
    loads[1].wait()
    magnitude = jnp.exp(-decay_v[...])
    lam_r = magnitude * jnp.cos(angle_v[...])
    lam_i = magnitude * jnp.sin(angle_v[...])

    def lanes(q):
        return slice(q * LANES, (q + 1) * LANES)

    def store_power(j, carry):
        pr, pi = carry
        for q in range(quarters):
            power[q, j, :MODES, :] = pr[:, lanes(q)]
            power[q, j, MODES:, :] = pi[:, lanes(q)]
        return cmul(pr, pi, lam_r, lam_i)

    pr, pi = lax.fori_loop(0, step, store_power, (jnp.ones_like(lam_r), jnp.zeros_like(lam_r)), unroll=4)
    for q in range(quarters):
        power[q, step, :MODES, :] = pr[:, lanes(q)]
        power[q, step, MODES:, :] = pi[:, lanes(q)]
        lam_block[q, :MODES, :] = pr[:, lanes(q)]
        lam_block[q, MODES:, :] = pi[:, lanes(q)]
    for _ in range(3):
        pr, pi = cmul(pr, pi, pr, pi)
    for q in range(quarters):
        lam_span[q, :MODES, :] = pr[:, lanes(q)]
        lam_span[q, MODES:, :] = pi[:, lanes(q)]
    for _ in range(2):
        pr, pi = cmul(pr, pi, pr, pi)
    for q in range(quarters):
        lam_row[q, :MODES, :] = pr[:, lanes(q)]
        lam_row[q, MODES:, :] = pi[:, lanes(q)]

    loads[2].wait()
    loads[3].wait()
    for q in range(quarters):
        u[q, : 8 * BLOCKS, :] = jnp.zeros((8 * BLOCKS, LANES), jnp.float32)
        for b in range(BLOCKS):
            part = slice(b * step, (b + 1) * step)
            drive = key_v[part, lanes(q)].astype(jnp.float32) * value_v[part, lanes(q)].astype(jnp.float32)
            u[q, pl.ds(8 * BLOCKS + b, step, stride=BLOCKS), :] = drive


    def total_of(i, _):
        q = lax.rem(x + jnp.where(i == 0, 2, jnp.where(i == 1, 1, jnp.where(i == 2, 3, 0))), NX)

        def add_token(j, acc):
            row = u[q, pl.ds(pl.multiple_of(8 * BLOCKS + j * BLOCKS, BLOCKS), BLOCKS), :]
            return tuple(acc[k] + power[q, step - 1 - j, pl.ds(k, 1), :] * row for k in range(STATE))

        acc = lax.fori_loop(
            0, step, add_token, tuple(jnp.zeros((BLOCKS, LANES), jnp.float32) for _ in range(STATE)), unroll=8
        )
        for k in range(STATE):
            sums[q, pl.ds(k, BLOCKS, stride=STATE), :] = acc[k]
        lam = lam_block[q]
        state = sums[q, :STATE, :]
        for b in range(1, BLOCKS):
            state = advanced(lam, state) + sums[q, b * STATE : (b + 1) * STATE, :]
        tot[q] = state

        @pl.when(i < NX - 1)
        def _():
            remote(
                tot.at[q], tot_in.at[x], tot_send.at[q], tot_recv.at[x], {"ctx": z * NX + q, "ch": ch}
            ).start()

        @pl.when(i == NX - 1)
        def _():
            tot_in[x] = state

        return 0

    lax.fori_loop(0, quarters, total_of, 0)

    for i in (4, 5, 6):
        loads[i].wait()
    for q in range(quarters):
        rr, ri = real_v[:, lanes(q)], imag_v[:, lanes(q)]
        taps[q, 0:1, :] = jnp.sum(rr, axis=0, keepdims=True) + skip_v[:, lanes(q)]

        def store_ker(j, _, q=q, rr=rr, ri=ri):
            p = power[q, j + 1]
            kr, ki = cmul(rr, ri, p[:MODES], p[MODES:])
            ker[q, j, :MODES, :] = kr
            ker[q, j, MODES:, :] = -ki
            taps[q, pl.ds(j + 1, 1), :] = jnp.sum(kr, axis=0, keepdims=True)
            return 0

        lax.fori_loop(0, step, store_ker, 0, unroll=4)

    for d in range(1, NX):
        src = lax.rem(x + d, NX)
        remote(tot.at[src], tot_in.at[src], tot_send.at[src], tot_recv.at[src], sibling).wait_recv()
    lam = lam_span[x]
    state = tot_in[0]
    for i in range(1, NX):
        state = advanced(lam, state) + tot_in[i]
    row_tot[...] = state.astype(row_tot.dtype)

    def row_copy(d):
        return remote(
            row_tot, row_in.at[z], row_send.at[d], row_recv.at[z], {"ctx": lax.rem(z + d, nz) * NX + x, "ch": ch}
        )

    def send_row(d):
        @pl.when(z + d < nz)
        def _():
            pl.semaphore_wait(ready.at[d], 1)
            row_copy(d).start()

    by_distance = sorted(range(1, nz), key=lambda d: (2 * d == nz, -min(d, nz - d), d))
    for d in by_distance[:-1]:
        send_row(d)

    loads[7].wait()
    chunk = 8 * BLOCKS

    def fir(q, _):
        for c in range(step // 8):
            acc = None
            for lag in range(8 * c + 8):
                begin = chunk + c * chunk - lag * BLOCKS
                term = taps[q, pl.ds(lag, 1), :] * u[q, begin : begin + chunk, :]
                acc = term if acc is None else acc + term
            local[q, c * chunk : (c + 1) * chunk, :] = acc
        return 0

    lax.fori_loop(0, quarters, fir, 0)
    for q in range(quarters):
        for b in range(BLOCKS):
            part = slice(b * step, (b + 1) * step)
            g_perm[q, pl.ds(b, step, stride=BLOCKS), :] = gate_v[part, lanes(q)].astype(jnp.float32)

    send_row(by_distance[-1])

    lam = lam_row[x]
    before[...] = jnp.zeros_like(before)
    for s in range(nz - 1):

        @pl.when(s < z)
        def _():
            remote(row_tot, row_in.at[s], row_send.at[0], row_recv.at[s], sibling).wait_recv()
            before[...] = advanced(lam, before[...]) + row_in[s].astype(jnp.float32)

    lam = lam_span[x]
    state = before[...]
    for i in range(NX):
        start_out[i] = state
        if i < NX - 1:
            state = advanced(lam, state) + tot_in[i]
    for d in (2, 1, 3):
        to = lax.rem(x + d, NX)
        remote(
            start_out.at[to], start_in.at[x], start_send.at[d], start_recv.at[x], {"ctx": z * NX + to, "ch": ch}
        ).start()
    start_in[x] = start_out[x]

    loads[8].wait()
    for to in range(NY):
        w_t[to, :width, :] = w_all[to, :, :width].T
    w_copy.wait_recv()
    for to in range(NY):
        w_t[to, width:, :] = w_all[to, :, width:].T

    def rows_of(g):
        begin = sum(GROUP_ROWS[:g])
        return slice(begin, begin + GROUP_ROWS[g])

    def halves_of(g):
        at = rows_of(g)
        middle = (at.start + at.stop) // 2
        return slice(at.start, middle), slice(middle, at.stop)

    def block_states(q):
        lam = lam_block[q]
        state = start_in[q]
        for b in range(BLOCKS):
            states[q, pl.ds(b, STATE, stride=BLOCKS), :] = state
            if b < BLOCKS - 1:
                state = advanced(lam, state) + sums[q, b * STATE : (b + 1) * STATE, :]

    def gated(g, some=tuple(range(quarters))):
        at_rows = rows_of(g)

        for q in some:
            to_lanes = pl.ds(pl.multiple_of(q * LANES, LANES), LANES)
            held = [states[q, k * BLOCKS : (k + 1) * BLOCKS, :] for k in range(STATE)]

            def two_tokens(i, _, q=q, held=held, to_lanes=to_lanes):
                done = []
                for t in range(2):
                    j = 2 * i + t
                    at = pl.ds(pl.multiple_of(j * BLOCKS, BLOCKS), BLOCKS)
                    partial = [local[q, at, :], None, None, None]
                    for k in range(STATE):
                        term = ker[q, j, pl.ds(k, 1), :] * held[k]
                        partial[k % 4] = term if partial[k % 4] is None else partial[k % 4] + term
                    total = (partial[0] + partial[1]) + (partial[2] + partial[3])
                    done.append(total * g_perm[q, at, :])
                to = pl.ds(pl.multiple_of(i * 2 * BLOCKS, 2 * BLOCKS), 2 * BLOCKS)
                g_all[to, to_lanes] = jnp.concatenate(done, axis=0).astype(jnp.bfloat16)
                return 0

            lax.fori_loop(at_rows.start // (2 * BLOCKS), at_rows.stop // (2 * BLOCKS), two_tokens, 0, unroll=4)

    def sib_copy(g):
        at = rows_of(g)
        return remote(g_all.at[at, :width], g_all.at[at, width:], gsib_send.at[g], gsib_recv.at[g], sibling)

    def product(g, to):
        return lax.dot_general(
            g_all[rows_of(g), :], w_t[to], (((1,), (0,)), ((), ())), preferred_element_type=jnp.float32
        )

    def far_copies(g):
        low, high = halves_of(g)
        return (
            remote(far_out.at[low], far_in.at[low], far_send.at[g, 0], far_recv.at[g, 0], up_dev),
            remote(far_out.at[high], far_in.at[high], far_send.at[g, 1], far_recv.at[g, 1], down_dev),
        )

    def up_copy(g, i):
        at = halves_of(g)[i]
        return remote(up_out.at[at], up_in.at[at], up_send.at[g, i], up_recv.at[g, i], up_dev)

    def down_copy(g, i):
        at = halves_of(g)[i]
        return remote(down_out.at[at], down_in.at[at], down_send.at[g, i], down_recv.at[g, i], down_dev)

    def send_off(g):
        low, high = halves_of(g)
        half = GROUP_ROWS[g] // 2
        far_out[rows_of(g), :] = product(g, y_far).astype(jnp.bfloat16)
        for copy in far_copies(g):
            copy.start()
        part = product(g, y_up)
        up_out[high, :] = part[half:].astype(jnp.bfloat16)
        up_copy(g, 1).start()
        up_part[low, :] = part[:half]
        part = product(g, y_down)
        down_out[low, :] = part[:half].astype(jnp.bfloat16)
        down_copy(g, 0).start()
        down_part[high, :] = part[half:]

    def send_rest(g):
        low, high = halves_of(g)
        arrived = far_copies(g)
        arrived[0].wait_recv()
        up_out[low, :] = (up_part[low, :] + far_in[low, :].astype(jnp.float32)).astype(jnp.bfloat16)
        up_copy(g, 0).start()
        arrived[1].wait_recv()
        down_out[high, :] = (down_part[high, :] + far_in[high, :].astype(jnp.float32)).astype(jnp.bfloat16)
        down_copy(g, 1).start()

    def keep_own(g):
        own_part[rows_of(g), :] = product(g, y)

    for d in (0, 1, 3, 2):
        q = lax.rem(x + d, NX)
        if d:
            remote(start_out.at[q], start_in.at[q], start_send.at[0], start_recv.at[q], sibling).wait_recv()
        block_states(q)
        for g in range(EARLY):
            gated(g, (q,))
    for g in range(EARLY):
        sib_copy(g).start()
    gated(1)
    sib_copy(1).start()
    for g in range(2):
        sib_copy(g).wait_recv()
        send_off(g)
    gated(2)
    sib_copy(2).start()
    send_rest(0)
    sib_copy(2).wait_recv()
    send_off(2)
    send_rest(1)
    send_rest(2)
    for g in range(GROUPS):
        keep_own(g)

    done = 0
    for g in range(GROUPS):
        for i in (1, 0):
            down_copy(g, 1 - i).wait_recv()
            up_copy(g, i).wait_recv()
        at = rows_of(g)
        whole = own_part[at, :] + up_in[at, :].astype(jnp.float32) + down_in[at, :].astype(jnp.float32)
        for q in range(quarters):
            final[q, at, :] = whole[:, lanes(q)]
        while at.stop - done >= 16 * BLOCKS:
            first = done // BLOCKS
            for q in range(quarters):
                for b in range(BLOCKS):
                    tokens = final[q, pl.ds(done + b, 16, stride=BLOCKS), :]
                    out[b * step + first : b * step + first + 16, lanes(q)] = tokens.astype(jnp.bfloat16)
            done += 16 * BLOCKS

    w_copy.wait_send()
    for d in range(1, NX):
        q = lax.rem(x + d, NX)
        remote(tot.at[q], tot_in.at[x], tot_send.at[q], tot_recv.at[x], sibling).wait_send()
        remote(start_out.at[q], start_in.at[x], start_send.at[d], start_recv.at[x], sibling).wait_send()
    for d in range(1, nz):

        @pl.when(z + d < nz)
        def _():
            row_copy(d).wait_send()

    for g in range(GROUPS):
        sib_copy(g).wait_send()
        for copy in far_copies(g):
            copy.wait_send()
        for i in range(2):
            up_copy(g, i).wait_send()
            down_copy(g, i).wait_send()


def per_device(
    gate_signal, key_signal, value_signal, pole_decay, pole_angle, residue_real, residue_imag, skip_gain, out_weight
):
    rows, width = key_signal.shape
    nz = lax.axis_size("ctx") // NX
    quarters = width // LANES
    step = rows // BLOCKS
    outs = out_weight.shape[0] // (2 * NY)
    weight = out_weight.reshape(NY, 2, outs, width)
    f32, bf16 = jnp.float32, jnp.bfloat16
    dma = pltpu.SemaphoreType.DMA

    def vmem(dtype, *shape):
        return pltpu.VMEM(shape, dtype)

    scratch = [
        vmem(bf16, rows, width),
        vmem(bf16, rows, width),
        vmem(bf16, rows, width),
        vmem(f32, MODES, width),
        vmem(f32, MODES, width),
        vmem(f32, MODES, width),
        vmem(f32, MODES, width),
        vmem(f32, 1, width),
        vmem(bf16, NY, outs, 2 * width),
        vmem(bf16, NY, 2 * width, outs),
        vmem(f32, quarters, 8 * BLOCKS + rows, LANES),
        vmem(f32, quarters, rows, LANES),
        vmem(f32, quarters, step + 1, STATE, LANES),
        vmem(f32, quarters, step, STATE, LANES),
        vmem(f32, quarters, step + 8, LANES),
        vmem(f32, quarters, STATE, LANES),
        vmem(f32, quarters, STATE, LANES),
        vmem(f32, quarters, STATE, LANES),
        vmem(f32, quarters, STATE * BLOCKS, LANES),
        vmem(f32, quarters, STATE, LANES),
        vmem(f32, NX, STATE, LANES),
        vmem(bf16, STATE, LANES),
        vmem(bf16, nz, STATE, LANES),
        vmem(f32, STATE, LANES),
        vmem(f32, NX, STATE, LANES),
        vmem(f32, NX, STATE, LANES),
        vmem(f32, quarters, STATE * BLOCKS, LANES),
        vmem(f32, quarters, rows, LANES),
        vmem(bf16, rows, 2 * width),
        vmem(bf16, rows, outs),
        vmem(bf16, rows, outs),
        vmem(bf16, rows, outs),
        vmem(bf16, rows, outs),
        vmem(bf16, rows, outs),
        vmem(bf16, rows, outs),
        vmem(f32, rows, outs),
        vmem(f32, rows, outs),
        vmem(f32, rows, outs),
        vmem(f32, outs // LANES, rows, LANES),
        dma((9,)),
        dma((2,)),
        dma((NX,)),
        dma((NX,)),
        dma((nz,)),
        dma((nz,)),
        dma((NX,)),
        dma((NX,)),
        dma((GROUPS,)),
        dma((GROUPS,)),
        dma((GROUPS, 2)),
        dma((GROUPS, 2)),
        dma((GROUPS, 2)),
        dma((GROUPS, 2)),
        dma((GROUPS, 2)),
        dma((GROUPS, 2)),
        pltpu.SemaphoreType.REGULAR((nz,)),
    ]
    hbm = pl.BlockSpec(memory_space=pltpu.HBM)
    return pl.pallas_call(
        functools.partial(kernel, nz),
        out_shape=jax.ShapeDtypeStruct((rows, outs), bf16),
        in_specs=[hbm] * 9,
        out_specs=pl.BlockSpec(memory_space=pltpu.VMEM),
        scratch_shapes=scratch,
        compiler_params=pltpu.CompilerParams(
            collective_id=0, has_side_effects=True, vmem_limit_bytes=48 * 1024 * 1024
        ),
    )(
        *(
            pltpu.with_memory_space_constraint(array, pltpu.HBM)
            for array in (
                gate_signal,
                key_signal,
                value_signal,
                pole_decay,
                pole_angle,
                residue_real,
                residue_imag,
                skip_gain.reshape(1, width),
                weight,
            )
        )
    )


def solution(mesh):
    return jax.shard_map(
        per_device,
        mesh=mesh,
        in_specs=(
            P("ctx", "ch"),
            P("ctx", "ch"),
            P("ctx", "ch"),
            P(None, "ch"),
            P(None, "ch"),
            P(None, "ch"),
            P(None, "ch"),
            P("ch"),
            P(None, "ch"),
        ),
        out_specs=P("ctx", "ch"),
        check_vma=False,
    )
```

```python
import functools

import jax
import jax.numpy as jnp
from jax import lax
from jax.experimental import pallas as pl
from jax.experimental.pallas import tpu as pltpu
from jax.sharding import PartitionSpec as P

MESH = pl.DeviceIdType.MESH
MODES = 16
STATE = 2 * MODES
LANES = 128
BLOCKS = 8
NX = 4
NY = 4
GROUP_ROWS = (64, 64, 128)
EARLY = 1
GROUPS = len(GROUP_ROWS)


def cmul(ar, ai, br, bi):
    return ar * br - ai * bi, ar * bi + ai * br


def half_turn(angle):
    half = 0.5 * angle
    square = half * half
    sine, cosine = 1.0, 1.0
    for n in range(6, 0, -1):
        sine = 1.0 - square * (1.0 / (2 * n * (2 * n + 1))) * sine
    for n in range(7, 0, -1):
        cosine = 1.0 - square * (1.0 / (2 * n * (2 * n - 1))) * cosine
    sine = half * sine
    return 2.0 * sine * cosine, (cosine - sine) * (cosine + sine)


def advanced(step, state):
    real, imag = cmul(step[:MODES], step[MODES:], state[:MODES], state[MODES:])
    return jnp.concatenate([real, imag], axis=0)


def kernel(
    nz,
    gate,
    key,
    value,
    decay,
    angle,
    res_real,
    res_imag,
    skip,
    weight,
    out,
    gate_v,
    key_v,
    value_v,
    decay_v,
    angle_v,
    real_v,
    imag_v,
    skip_v,
    w_all,
    w_t,
    u,
    g_perm,
    power,
    ker,
    taps,
    lam_block,
    lam_span,
    lam_row,
    sums,
    tot,
    tot_in,
    row_tot,
    row_in,
    before,
    start_out,
    start_in,
    states,
    local,
    g_all,
    far_out,
    far_in,
    up_out,
    up_in,
    down_out,
    down_in,
    up_part,
    down_part,
    own_part,
    final,
    load_sem,
    wsib_sem,
    tot_send,
    tot_recv,
    row_send,
    row_recv,
    start_send,
    start_recv,
    gsib_send,
    gsib_recv,
    far_send,
    far_recv,
    up_send,
    up_recv,
    down_send,
    down_recv,
    ready,
):
    rows, width = key_v.shape
    step = rows // BLOCKS
    quarters = width // LANES
    ctx, ch = lax.axis_index("ctx"), lax.axis_index("ch")
    z, x = ctx // NX, lax.rem(ctx, NX)
    y, core = ch // 2, lax.rem(ch, 2)
    sibling = {"ctx": ctx, "ch": y * 2 + (1 - core)}
    y_up, y_down, y_far = (lax.rem(y + d, NY) for d in (1, NY - 1, 2))
    up_dev = {"ctx": ctx, "ch": y_up * 2 + core}
    down_dev = {"ctx": ctx, "ch": y_down * 2 + core}

    def remote(src, dst, send, recv, device):
        return pltpu.make_async_remote_copy(
            src_ref=src, dst_ref=dst, send_sem=send, recv_sem=recv, device_id=device, device_id_type=MESH
        )

    pairs = (
        (decay, decay_v),
        (angle, angle_v),
        (key, key_v),
        (value, value_v),
        (res_real, real_v),
        (res_imag, imag_v),
        (skip, skip_v),
        (gate, gate_v),
        (weight.at[:, core], w_all.at[:, :, :width]),
    )
    loads = [pltpu.make_async_copy(src, dst, load_sem.at[i]) for i, (src, dst) in enumerate(pairs)]
    for load in loads:
        load.start()

    barrier = pltpu.get_barrier_semaphore()
    peers = [sibling, up_dev, down_dev]
    peers += [{"ctx": z * NX + lax.rem(x + d, NX), "ch": ch} for d in range(1, NX)]
    for peer in peers:
        pl.semaphore_signal(barrier, inc=1, device_id=peer, device_id_type=MESH)
    for d in range(1, nz):

        @pl.when(z + d < nz)
        def _():
            later = {"ctx": (z + d) * NX + x, "ch": ch}
            pl.semaphore_signal(barrier, inc=1, device_id=later, device_id_type=MESH)

    pl.semaphore_wait(barrier, len(peers) + z)
    for d in range(1, nz):

        @pl.when(z >= d)
        def _():
            earlier = {"ctx": (z - d) * NX + x, "ch": ch}
            pl.semaphore_signal(ready.at[d], inc=1, device_id=earlier, device_id_type=MESH)

    w_copy = remote(weight.at[:, 1 - core], w_all.at[:, :, width:], wsib_sem.at[0], wsib_sem.at[1], sibling)
    w_copy.start()

    loads[0].wait()
    loads[1].wait()
    magnitude = jnp.exp(-decay_v[...])
    sine, cosine = half_turn(angle_v[...])
    lam_r = magnitude * cosine
    lam_i = magnitude * sine

    def lanes(q):
        return slice(q * LANES, (q + 1) * LANES)

    def store_power(j, carry):
        pr, pi = carry
        for q in range(quarters):
            power[q, j, :MODES, :] = pr[:, lanes(q)]
            power[q, j, MODES:, :] = pi[:, lanes(q)]
        return cmul(pr, pi, lam_r, lam_i)

    pr, pi = lax.fori_loop(0, step, store_power, (jnp.ones_like(lam_r), jnp.zeros_like(lam_r)), unroll=4)
    for q in range(quarters):
        power[q, step, :MODES, :] = pr[:, lanes(q)]
        power[q, step, MODES:, :] = pi[:, lanes(q)]
        lam_block[q, :MODES, :] = pr[:, lanes(q)]
        lam_block[q, MODES:, :] = pi[:, lanes(q)]
    for _ in range(3):
        pr, pi = cmul(pr, pi, pr, pi)
    for q in range(quarters):
        lam_span[q, :MODES, :] = pr[:, lanes(q)]
        lam_span[q, MODES:, :] = pi[:, lanes(q)]
    for _ in range(2):
        pr, pi = cmul(pr, pi, pr, pi)
    for q in range(quarters):
        lam_row[q, :MODES, :] = pr[:, lanes(q)]
        lam_row[q, MODES:, :] = pi[:, lanes(q)]

    loads[2].wait()
    loads[3].wait()
    for q in range(quarters):
        u[q, : 8 * BLOCKS, :] = jnp.zeros((8 * BLOCKS, LANES), jnp.float32)
        for b in range(BLOCKS):
            part = slice(b * step, (b + 1) * step)
            drive = key_v[part, lanes(q)].astype(jnp.float32) * value_v[part, lanes(q)].astype(jnp.float32)
            u[q, pl.ds(8 * BLOCKS + b, step, stride=BLOCKS), :] = drive


    def total_of(i, _):
        q = lax.rem(x + jnp.where(i == 0, 2, jnp.where(i == 1, 1, jnp.where(i == 2, 3, 0))), NX)

        def add_token(j, acc):
            row = u[q, pl.ds(pl.multiple_of(8 * BLOCKS + j * BLOCKS, BLOCKS), BLOCKS), :]
            return tuple(acc[k] + power[q, step - 1 - j, pl.ds(k, 1), :] * row for k in range(STATE))

        acc = lax.fori_loop(
            0, step, add_token, tuple(jnp.zeros((BLOCKS, LANES), jnp.float32) for _ in range(STATE)), unroll=32
        )
        for k in range(STATE):
            sums[q, pl.ds(k, BLOCKS, stride=STATE), :] = acc[k]
        lam = lam_block[q]
        state = sums[q, :STATE, :]
        for b in range(1, BLOCKS):
            state = advanced(lam, state) + sums[q, b * STATE : (b + 1) * STATE, :]
        tot[q] = state

        @pl.when(i < NX - 1)
        def _():
            remote(
                tot.at[q], tot_in.at[x], tot_send.at[q], tot_recv.at[x], {"ctx": z * NX + q, "ch": ch}
            ).start()

        @pl.when(i == NX - 1)
        def _():
            tot_in[x] = state

        return 0

    lax.fori_loop(0, quarters, total_of, 0)

    for i in (4, 5, 6):
        loads[i].wait()
    for q in range(quarters):
        rr, ri = real_v[:, lanes(q)], imag_v[:, lanes(q)]
        taps[q, 0:1, :] = jnp.sum(rr, axis=0, keepdims=True) + skip_v[:, lanes(q)]

        def store_ker(j, _, q=q, rr=rr, ri=ri):
            p = power[q, j + 1]
            kr, ki = cmul(rr, ri, p[:MODES], p[MODES:])
            ker[q, j, :MODES, :] = kr
            ker[q, j, MODES:, :] = -ki
            taps[q, pl.ds(j + 1, 1), :] = jnp.sum(kr, axis=0, keepdims=True)
            return 0

        lax.fori_loop(0, step, store_ker, 0, unroll=4)

    for d in range(1, NX):
        src = lax.rem(x + d, NX)
        remote(tot.at[src], tot_in.at[src], tot_send.at[src], tot_recv.at[src], sibling).wait_recv()
    lam = lam_span[x]
    state = tot_in[0]
    for i in range(1, NX):
        state = advanced(lam, state) + tot_in[i]
    row_tot[...] = state.astype(row_tot.dtype)

    def row_copy(d):
        return remote(
            row_tot, row_in.at[z], row_send.at[d], row_recv.at[z], {"ctx": lax.rem(z + d, nz) * NX + x, "ch": ch}
        )

    def send_row(d):
        @pl.when(z + d < nz)
        def _():
            pl.semaphore_wait(ready.at[d], 1)
            row_copy(d).start()

    by_distance = sorted(range(1, nz), key=lambda d: (2 * d == nz, -min(d, nz - d), d))
    for d in by_distance[:-1]:
        send_row(d)

    loads[7].wait()
    chunk = 8 * BLOCKS

    def fir(q, _):
        for c in range(step // 8):
            acc = None
            for lag in range(8 * c + 8):
                begin = chunk + c * chunk - lag * BLOCKS
                term = taps[q, pl.ds(lag, 1), :] * u[q, begin : begin + chunk, :]
                acc = term if acc is None else acc + term
            local[q, c * chunk : (c + 1) * chunk, :] = acc
        return 0

    for q in range(quarters):
        for b in range(BLOCKS):
            part = slice(b * step, (b + 1) * step)
            g_perm[q, pl.ds(b, step, stride=BLOCKS), :] = gate_v[part, lanes(q)].astype(jnp.float32)

    loads[8].wait()
    for to in range(NY):
        w_t[to, :width, :] = w_all[to, :, :width].T
    send_row(by_distance[-1])

    lam = lam_row[x]
    before[...] = jnp.zeros_like(before)
    for s in range(nz - 1):

        @pl.when(s < z)
        def _():
            remote(row_tot, row_in.at[s], row_send.at[0], row_recv.at[s], sibling).wait_recv()
            before[...] = advanced(lam, before[...]) + row_in[s].astype(jnp.float32)

    lam = lam_span[x]
    state = before[...]
    for i in range(NX):
        start_out[i] = state
        if i < NX - 1:
            state = advanced(lam, state) + tot_in[i]
    for d in (2, 1, 3):
        to = lax.rem(x + d, NX)
        remote(
            start_out.at[to], start_in.at[x], start_send.at[d], start_recv.at[x], {"ctx": z * NX + to, "ch": ch}
        ).start()
    start_in[x] = start_out[x]

    lax.fori_loop(0, quarters, fir, 0)

    w_copy.wait_recv()
    for to in range(NY):
        w_t[to, width:, :] = w_all[to, :, width:].T

    def rows_of(g):
        begin = sum(GROUP_ROWS[:g])
        return slice(begin, begin + GROUP_ROWS[g])

    def halves_of(g):
        at = rows_of(g)
        middle = (at.start + at.stop) // 2
        return slice(at.start, middle), slice(middle, at.stop)

    def block_states(q):
        lam = lam_block[q]
        state = start_in[q]
        for b in range(BLOCKS):
            states[q, pl.ds(b, STATE, stride=BLOCKS), :] = state
            if b < BLOCKS - 1:
                state = advanced(lam, state) + sums[q, b * STATE : (b + 1) * STATE, :]

    def gated(g, some=tuple(range(quarters))):
        at_rows = rows_of(g)

        for q in some:
            to_lanes = pl.ds(pl.multiple_of(q * LANES, LANES), LANES)
            held = [states[q, k * BLOCKS : (k + 1) * BLOCKS, :] for k in range(STATE)]

            def two_tokens(i, _, q=q, held=held, to_lanes=to_lanes):
                done = []
                for t in range(2):
                    j = 2 * i + t
                    at = pl.ds(pl.multiple_of(j * BLOCKS, BLOCKS), BLOCKS)
                    partial = [local[q, at, :], None, None, None]
                    for k in range(STATE):
                        term = ker[q, j, pl.ds(k, 1), :] * held[k]
                        partial[k % 4] = term if partial[k % 4] is None else partial[k % 4] + term
                    total = (partial[0] + partial[1]) + (partial[2] + partial[3])
                    done.append(total * g_perm[q, at, :])
                to = pl.ds(pl.multiple_of(i * 2 * BLOCKS, 2 * BLOCKS), 2 * BLOCKS)
                g_all[to, to_lanes] = jnp.concatenate(done, axis=0).astype(jnp.bfloat16)
                return 0

            lax.fori_loop(at_rows.start // (2 * BLOCKS), at_rows.stop // (2 * BLOCKS), two_tokens, 0, unroll=4)

    def sib_copy(g):
        at = rows_of(g)
        return remote(g_all.at[at, :width], g_all.at[at, width:], gsib_send.at[g], gsib_recv.at[g], sibling)

    def product(g, to):
        return lax.dot_general(
            g_all[rows_of(g), :], w_t[to], (((1,), (0,)), ((), ())), preferred_element_type=jnp.float32
        )

    def far_copies(g):
        low, high = halves_of(g)
        return (
            remote(far_out.at[low], far_in.at[low], far_send.at[g, 0], far_recv.at[g, 0], up_dev),
            remote(far_out.at[high], far_in.at[high], far_send.at[g, 1], far_recv.at[g, 1], down_dev),
        )

    def up_copy(g, i):
        at = halves_of(g)[i]
        return remote(up_out.at[at], up_in.at[at], up_send.at[g, i], up_recv.at[g, i], up_dev)

    def down_copy(g, i):
        at = halves_of(g)[i]
        return remote(down_out.at[at], down_in.at[at], down_send.at[g, i], down_recv.at[g, i], down_dev)

    def send_off(g):
        low, high = halves_of(g)
        half = GROUP_ROWS[g] // 2
        far_out[rows_of(g), :] = product(g, y_far).astype(jnp.bfloat16)
        for copy in far_copies(g):
            copy.start()
        part = product(g, y_up)
        up_out[high, :] = part[half:].astype(jnp.bfloat16)
        up_copy(g, 1).start()
        up_part[low, :] = part[:half]
        part = product(g, y_down)
        down_out[low, :] = part[:half].astype(jnp.bfloat16)
        down_copy(g, 0).start()
        down_part[high, :] = part[half:]

    def send_rest(g):
        low, high = halves_of(g)
        arrived = far_copies(g)
        arrived[0].wait_recv()
        up_out[low, :] = (up_part[low, :] + far_in[low, :].astype(jnp.float32)).astype(jnp.bfloat16)
        up_copy(g, 0).start()
        arrived[1].wait_recv()
        down_out[high, :] = (down_part[high, :] + far_in[high, :].astype(jnp.float32)).astype(jnp.bfloat16)
        down_copy(g, 1).start()

    def keep_own(g):
        own_part[rows_of(g), :] = product(g, y)

    for d in (0, 1, 3, 2):
        q = lax.rem(x + d, NX)
        if d:
            remote(start_out.at[q], start_in.at[q], start_send.at[0], start_recv.at[q], sibling).wait_recv()
        block_states(q)
        for g in range(EARLY):
            gated(g, (q,))
    for g in range(EARLY):
        sib_copy(g).start()
    gated(1)
    sib_copy(1).start()
    for g in range(2):
        sib_copy(g).wait_recv()
        send_off(g)
    gated(2)
    sib_copy(2).start()
    send_rest(0)
    sib_copy(2).wait_recv()
    send_off(2)
    send_rest(1)
    send_rest(2)
    for g in range(GROUPS):
        keep_own(g)

    done = 0
    for g in range(GROUPS):
        for i in (1, 0):
            down_copy(g, 1 - i).wait_recv()
            up_copy(g, i).wait_recv()
        at = rows_of(g)
        whole = own_part[at, :] + up_in[at, :].astype(jnp.float32) + down_in[at, :].astype(jnp.float32)
        for q in range(quarters):
            final[q, at, :] = whole[:, lanes(q)]
        while at.stop - done >= 16 * BLOCKS:
            first = done // BLOCKS
            for q in range(quarters):
                for b in range(BLOCKS):
                    tokens = final[q, pl.ds(done + b, 16, stride=BLOCKS), :]
                    out[b * step + first : b * step + first + 16, lanes(q)] = tokens.astype(jnp.bfloat16)
            done += 16 * BLOCKS

    w_copy.wait_send()
    for d in range(1, NX):
        q = lax.rem(x + d, NX)
        remote(tot.at[q], tot_in.at[x], tot_send.at[q], tot_recv.at[x], sibling).wait_send()
        remote(start_out.at[q], start_in.at[x], start_send.at[d], start_recv.at[x], sibling).wait_send()
    for d in range(1, nz):

        @pl.when(z + d < nz)
        def _():
            row_copy(d).wait_send()

    for g in range(GROUPS):
        sib_copy(g).wait_send()
        for copy in far_copies(g):
            copy.wait_send()
        for i in range(2):
            up_copy(g, i).wait_send()
            down_copy(g, i).wait_send()


def per_device(
    gate_signal, key_signal, value_signal, pole_decay, pole_angle, residue_real, residue_imag, skip_gain, out_weight
):
    rows, width = key_signal.shape
    nz = lax.axis_size("ctx") // NX
    quarters = width // LANES
    step = rows // BLOCKS
    outs = out_weight.shape[0] // (2 * NY)
    weight = out_weight.reshape(NY, 2, outs, width)
    f32, bf16 = jnp.float32, jnp.bfloat16
    dma = pltpu.SemaphoreType.DMA

    def vmem(dtype, *shape):
        return pltpu.VMEM(shape, dtype)

    scratch = [
        vmem(bf16, rows, width),
        vmem(bf16, rows, width),
        vmem(bf16, rows, width),
        vmem(f32, MODES, width),
        vmem(f32, MODES, width),
        vmem(f32, MODES, width),
        vmem(f32, MODES, width),
        vmem(f32, 1, width),
        vmem(bf16, NY, outs, 2 * width),
        vmem(bf16, NY, 2 * width, outs),
        vmem(f32, quarters, 8 * BLOCKS + rows, LANES),
        vmem(f32, quarters, rows, LANES),
        vmem(f32, quarters, step + 1, STATE, LANES),
        vmem(f32, quarters, step, STATE, LANES),
        vmem(f32, quarters, step + 8, LANES),
        vmem(f32, quarters, STATE, LANES),
        vmem(f32, quarters, STATE, LANES),
        vmem(f32, quarters, STATE, LANES),
        vmem(f32, quarters, STATE * BLOCKS, LANES),
        vmem(f32, quarters, STATE, LANES),
        vmem(f32, NX, STATE, LANES),
        vmem(bf16, STATE, LANES),
        vmem(bf16, nz, STATE, LANES),
        vmem(f32, STATE, LANES),
        vmem(f32, NX, STATE, LANES),
        vmem(f32, NX, STATE, LANES),
        vmem(f32, quarters, STATE * BLOCKS, LANES),
        vmem(f32, quarters, rows, LANES),
        vmem(bf16, rows, 2 * width),
        vmem(bf16, rows, outs),
        vmem(bf16, rows, outs),
        vmem(bf16, rows, outs),
        vmem(bf16, rows, outs),
        vmem(bf16, rows, outs),
        vmem(bf16, rows, outs),
        vmem(f32, rows, outs),
        vmem(f32, rows, outs),
        vmem(f32, rows, outs),
        vmem(f32, outs // LANES, rows, LANES),
        dma((9,)),
        dma((2,)),
        dma((NX,)),
        dma((NX,)),
        dma((nz,)),
        dma((nz,)),
        dma((NX,)),
        dma((NX,)),
        dma((GROUPS,)),
        dma((GROUPS,)),
        dma((GROUPS, 2)),
        dma((GROUPS, 2)),
        dma((GROUPS, 2)),
        dma((GROUPS, 2)),
        dma((GROUPS, 2)),
        dma((GROUPS, 2)),
        pltpu.SemaphoreType.REGULAR((nz,)),
    ]
    hbm = pl.BlockSpec(memory_space=pltpu.HBM)
    return pl.pallas_call(
        functools.partial(kernel, nz),
        out_shape=jax.ShapeDtypeStruct((rows, outs), bf16),
        in_specs=[hbm] * 9,
        out_specs=pl.BlockSpec(memory_space=pltpu.VMEM),
        scratch_shapes=scratch,
        compiler_params=pltpu.CompilerParams(
            collective_id=0, has_side_effects=True, vmem_limit_bytes=48 * 1024 * 1024
        ),
    )(
        *(
            pltpu.with_memory_space_constraint(array, pltpu.HBM)
            for array in (
                gate_signal,
                key_signal,
                value_signal,
                pole_decay,
                pole_angle,
                residue_real,
                residue_imag,
                skip_gain.reshape(1, width),
                weight,
            )
        )
    )


def solution(mesh):
    return jax.shard_map(
        per_device,
        mesh=mesh,
        in_specs=(
            P("ctx", "ch"),
            P("ctx", "ch"),
            P("ctx", "ch"),
            P(None, "ch"),
            P(None, "ch"),
            P(None, "ch"),
            P(None, "ch"),
            P("ch"),
            P(None, "ch"),
        ),
        out_specs=P("ctx", "ch"),
        check_vma=False,
    )
```
